32 devices in a mesh: adapter: 4 (over z), mp: 8 (over y, x, core).
Axes of the slice: x: 2, y: 2, z: 4, core: 2. Of those that a mesh axis runs over, the one named last changes fastest.
Arguments:
- tokens: bfloat16 [1536, 8192], P('adapter', 'mp'), may hold values from -6 to 6
- cotangent: bfloat16 [1536, 1024], P('adapter', 'mp'), may hold values from -6 to 6
- value_weight: bfloat16 [8192, 1024], P('mp', 'adapter'), may hold values from -0.0625 to 0.0625
- down_store: bfloat16 [8, 8, 1024, 64], P(None, 'mp', 'adapter'), may hold values from -0.0625 to 0.0625
- down_first: float32 [8, 8, 1024, 64], P(None, 'mp', 'adapter'), may hold values from -4 to 4
- down_second: float32 [8, 8, 1024, 64], P(None, 'mp', 'adapter'), may hold values from 0.01 to 1
- up_store: bfloat16 [8, 64, 1024], P(None, 'adapter', 'mp'), may hold values from -0.75 to 0.75
- up_first: float32 [8, 64, 1024], P(None, 'adapter', 'mp'), may hold values from -4 to 4
- up_second: float32 [8, 64, 1024], P(None, 'adapter', 'mp'), may hold values from 0.01 to 1
- tile_adapter: int32 [12], replicated, may hold values from 0 to 7
- tile_length: int32 [12], replicated, may hold values from 1 to 128, as said below
- adapter_slot: int32 [8], replicated, may hold values from 0 to 7, each once
Outputs:
- projected: bfloat16 [1536, 1024], P('adapter', 'mp')
- token_gradient: bfloat16 [1536, 8192], P('adapter', 'mp')
- new_down: float32 [8, 8, 1024, 64], P(None, 'mp', 'adapter')
- new_down_first: float32 [8, 8, 1024, 64], P(None, 'mp', 'adapter')
- new_down_second: float32 [8, 8, 1024, 64], P(None, 'mp', 'adapter')
- new_up: float32 [8, 64, 1024], P(None, 'adapter', 'mp')
- new_up_first: float32 [8, 64, 1024], P(None, 'adapter', 'mp')
- new_up_second: float32 [8, 64, 1024], P(None, 'adapter', 'mp')
The draws below stay inside these ranges and needn't reach their ends.
Inputs may be any that keep to these rules, and one draw needn't show every extreme that they name: `tile_length`: some tile is full in every draw. `adapter_slot`: each slot holds exactly one adapter.
All inputs are finite; a program needn't handle non-finite values.
Results may differ from the reference program's by a relative error of at most 0.0046.
Values may be sent and summed in bfloat16 or wider, within the bound.
A program may use at most 64 MiB of HBM per device.

```python
import math
import jax
import jax.numpy as jnp
import numpy as np
from jax import lax

MODEL_WIDTH = 8192
VALUE_OUTPUTS = 1024
R = 64
TILE = 128
STEP = 100
ADAPTERS = 8
TOKEN_TOTAL = 1536
N_TILES = 12
N_MP = 8


def draw_tile_length(key, part):
    first_key, second_key = jax.random.split(jax.random.fold_in(key, 11))
    lengths = jax.random.randint(first_key, (N_TILES,), 1, TILE + 1)
    full_tile = jax.random.randint(second_key, (), 0, N_TILES)
    return jnp.where(jnp.arange(N_TILES) == full_tile, TILE, lengths).astype(jnp.int32)


def set_ends(array, rng, smallest, top_value):
    longest = array.shape.index(max(array.shape))
    spots = []
    for shift in (0, 1):
        where = [jax.random.randint(jax.random.fold_in(rng, axis), (), 0, length) for axis, length in enumerate(array.shape)]
        where[longest] = (where[longest] + shift) % array.shape[longest]
        spots.append(tuple(where))
    return array.at[spots[0]].set(smallest).at[spots[1]].set(top_value)


def shard_levels(key, shape, cuts, low, high):
    def one(dim, blocks):
        draws = jax.random.uniform(jax.random.fold_in(jax.random.fold_in(key, 6), dim), (blocks,), jnp.float32, low / len(cuts), high / len(cuts))
        return jnp.repeat(jnp.exp(draws), shape[dim] // blocks).reshape((-1,) + (1,) * (len(shape) - dim - 1))

    factor_of = one(*cuts[0])
    for cut in cuts[1:]:
        factor_of = factor_of * one(*cut)
    return factor_of


def rank_table(amount, lean):
    portions = [(1 << 20) // math.isqrt(standing ** lean) + 1 for standing in range(1, amount + 1)]
    deviation = 1 + sum(portions) // (1 << 30)
    return np.cumsum(np.array([max(1, weight // deviation) for weight in portions]))


def ranked(stream_key, shape, count, lean):
    table = rank_table(count, lean)
    lot = jax.random.randint(jax.random.fold_in(stream_key, 1), shape, 0, int(table[count - 1]))
    standing = jnp.searchsorted(jnp.asarray(table, jnp.int32), lot, side="right")
    return jax.random.permutation(jax.random.fold_in(stream_key, 2), count)[standing].astype(jnp.int32)


def scatter_about(stream_key, shape, spread, limit, cuts=(), kind=jnp.bfloat16):
    array = jax.random.normal(stream_key, shape, jnp.float32) * spread
    if len(cuts) > 0:
        array = shard_levels(stream_key, shape, cuts, -0.22, 0.18) * array
    return jnp.clip(array, min=-limit, max=limit).astype(kind)


def setup_inputs(seed: int = 0) -> dict:
    key_list = jax.random.split(jax.random.key(seed), 13)
    tokens = scatter_about(key_list[0], (TOKEN_TOTAL, MODEL_WIDTH), 1.0, 6.0, ((0, 4), (1, 8)))
    cotangent = scatter_about(key_list[1], (TOKEN_TOTAL, VALUE_OUTPUTS), 1.0, 6.0, ((0, 4), (1, 8)))
    value_weight = scatter_about(key_list[2], (MODEL_WIDTH, VALUE_OUTPUTS), MODEL_WIDTH ** -0.5, 0.0625, ((0, 8), (1, 4)))
    down_store = scatter_about(key_list[3], (ADAPTERS, N_MP, MODEL_WIDTH // N_MP, R), MODEL_WIDTH ** -0.5, 0.0625, ((1, 8), (2, 4)))
    down_first = scatter_about(key_list[4], (ADAPTERS, N_MP, MODEL_WIDTH // N_MP, R), 0.3, 4.0, ((1, 8), (2, 4)), jnp.float32)
    down_second = jnp.clip(jnp.exp(math.log(1.0) - 4.6051702 * jax.random.uniform(key_list[5], (ADAPTERS, N_MP, MODEL_WIDTH // N_MP, R), jnp.float32) ** shard_levels(key_list[5], (ADAPTERS, N_MP, MODEL_WIDTH // N_MP, R), ((1, 8), (2, 4)), -0.2, 0.2)), 0.01, 1.0)
    up_store = scatter_about(key_list[6], (ADAPTERS, R, VALUE_OUTPUTS), R ** -0.5, 0.75, ((1, 4), (2, 8)))
    up_first = scatter_about(key_list[7], (ADAPTERS, R, VALUE_OUTPUTS), 0.3, 4.0, ((1, 4), (2, 8)), jnp.float32)
    up_second = jnp.clip(jnp.exp(math.log(1.0) - 4.6051702 * jax.random.uniform(key_list[8], (ADAPTERS, R, VALUE_OUTPUTS), jnp.float32) ** shard_levels(key_list[8], (ADAPTERS, R, VALUE_OUTPUTS), ((1, 4), (2, 8)), -0.2, 0.2)), 0.01, 1.0)
    tile_adapter = set_ends(ranked(key_list[9], (N_TILES,), ADAPTERS, 2), jax.random.fold_in(key_list[9], 3), 0, ADAPTERS - 1).astype(jnp.int32)
    tile_length = draw_tile_length(jax.random.fold_in(key_list[12], 71), 0)
    adapter_slot = jax.random.permutation(key_list[11], ADAPTERS).astype(jnp.int32)
    return dict(tokens=tokens, cotangent=cotangent, value_weight=value_weight, down_store=down_store, down_first=down_first, down_second=down_second, up_store=up_store, up_first=up_first, up_second=up_second, tile_adapter=tile_adapter, tile_length=tile_length, adapter_slot=adapter_slot)


adapter_scale = 2.0
learn_rate = 0.001
beta_one = 0.9
beta_two = 0.999
adam_eps = 1e-08

def adam_step(store, first, second, gradient):
    new_first = beta_one * first + (1.0 - beta_one) * gradient
    new_second = beta_two * second + (1.0 - beta_two) * gradient * gradient
    corr_one = 1.0 - beta_one ** STEP
    corr_two = 1.0 - beta_two ** STEP
    moved = store.astype(jnp.float32) - learn_rate * (new_first / corr_one) / (jnp.sqrt(new_second / corr_two) + adam_eps)
    return (moved, new_first, new_second)

def reference(tokens, cotangent, value_weight, down_store, down_first, down_second, up_store, up_first, up_second, tile_adapter, tile_length, adapter_slot):
    down_all = down_store.reshape(ADAPTERS, MODEL_WIDTH, R)
    tile_adapter_slot = adapter_slot[tile_adapter].astype(jnp.int32)
    position = jnp.arange(TILE)
    active_rows = (position[None, :] < tile_length[:, None]).reshape(TOKEN_TOTAL, 1)
    masked = cotangent * active_rows.astype(jnp.bfloat16)
    frozen_value = jnp.dot(tokens, value_weight, preferred_element_type=jnp.float32)
    frozen_backward = jnp.dot(masked, value_weight.T, preferred_element_type=jnp.float32)
    token_tiles = tokens.reshape(N_TILES, TILE, MODEL_WIDTH)
    tile_mask = masked.reshape(N_TILES, TILE, VALUE_OUTPUTS)

    def tile_values(carry, item):
        down_gradient, up_gradient = carry
        tok_rows, row_mask, slot_index = item
        down_weight = down_all[slot_index]
        up_weight = up_store[slot_index]
        down_portion = jnp.dot(tok_rows, down_weight, preferred_element_type=jnp.float32).astype(jnp.bfloat16)
        adapter_term = jnp.dot(down_portion, up_weight, preferred_element_type=jnp.float32)
        backward_portion = (adapter_scale * jnp.dot(row_mask, up_weight.T, preferred_element_type=jnp.float32)).astype(jnp.bfloat16)
        adapter_backward = jnp.dot(backward_portion, down_weight.T, preferred_element_type=jnp.float32)
        tile_down = jnp.dot(tok_rows.T, backward_portion, preferred_element_type=jnp.float32)
        tile_up_weight = adapter_scale * jnp.dot(down_portion.T, row_mask, preferred_element_type=jnp.float32)
        down_gradient = down_gradient.at[slot_index].add(tile_down)
        up_gradient = up_gradient.at[slot_index].add(tile_up_weight)
        return ((down_gradient, up_gradient), (adapter_term, adapter_backward))
    initial_down = jnp.zeros((ADAPTERS, MODEL_WIDTH, R), jnp.float32)
    initial_up = jnp.zeros((ADAPTERS, R, VALUE_OUTPUTS), jnp.float32)
    (down_gradient, up_gradient), (adapter_terms, adapter_backwards) = lax.scan(tile_values, (initial_down, initial_up), (token_tiles, tile_mask, tile_adapter_slot))
    projected = ((frozen_value + adapter_scale * adapter_terms.reshape(TOKEN_TOTAL, VALUE_OUTPUTS)) * active_rows.astype(jnp.float32)).astype(jnp.bfloat16)
    token_gradient = (frozen_backward + adapter_backwards.reshape(TOKEN_TOTAL, MODEL_WIDTH)).astype(jnp.bfloat16)
    new_down, new_down_first, new_down_second = adam_step(down_store, down_first, down_second, down_gradient.reshape(down_store.shape))
    new_up, new_up_first, new_up_second = adam_step(up_store, up_first, up_second, up_gradient)
    return (projected, token_gradient, new_down, new_down_first, new_down_second, new_up, new_up_first, new_up_second)
```

```python
import functools

import jax
import jax.numpy as jnp
from jax import lax
from jax.experimental import pallas as pl
from jax.experimental.pallas import tpu as pltpu
from jax.sharding import PartitionSpec as P

TILE = 128
STEP = 100


adapter_scale = 2.0
learn_rate = 0.001
beta_one = 0.9
beta_two = 0.999
adam_eps = 1e-08


def adam_step(store, first, second, gradient):
    new_first = beta_one * first + (1.0 - beta_one) * gradient
    new_second = beta_two * second + (1.0 - beta_two) * gradient * gradient
    corr_one = 1.0 - beta_one**STEP
    corr_two = 1.0 - beta_two**STEP
    moved = store.astype(jnp.float32) - learn_rate * (new_first / corr_one) / (
        jnp.sqrt(new_second / corr_two) + adam_eps
    )
    return (moved, new_first, new_second)


def shards(
    tokens,
    cotangent,
    value_weight,
    down_store,
    down_first,
    down_second,
    up_store,
    up_first,
    up_second,
    tile_adapter,
    tile_length,
    adapter_slot,
):
    tile_total = tile_adapter.shape[0]
    tok_count, feat_part = tokens.shape
    head_cols = cotangent.shape[1]
    tiles_here = tok_count // TILE
    adapter_count = adapter_slot.shape[0]
    my_index = lax.axis_index("adapter")
    adapter_ids = jnp.arange(adapter_count, dtype=jnp.int32)
    tile_adapter_slot = jnp.sum(
        jnp.where(tile_adapter[:, None] == adapter_ids[None, :], adapter_slot[None, :], 0), axis=1
    )
    my_lengths = lax.dynamic_slice_in_dim(tile_length, my_index * tiles_here, tiles_here)
    active_rows = (jnp.arange(TILE)[None, :] < my_lengths[:, None]).reshape(tok_count, 1)
    masked_own = cotangent * active_rows.astype(jnp.bfloat16)
    masked_full = lax.all_gather(masked_own, "mp", axis=1, tiled=True)
    sent_down = down_store[:, 0][tile_adapter_slot]
    sent_up = up_store[tile_adapter_slot]
    down_panel, up_panel = (
        lax.all_to_all(sent_down, "adapter", split_axis=0, concat_axis=1, tiled=True),
        lax.all_to_all(sent_up, "adapter", split_axis=0, concat_axis=1, tiled=True),
    )
    token_tiles = tokens.reshape(tiles_here, TILE, feat_part)
    frozen_part = jnp.dot(
        tokens,
        lax.all_gather(value_weight, "adapter", axis=1, tiled=True),
        preferred_element_type=jnp.float32,
    )
    frozen_local = lax.psum_scatter(frozen_part, "mp", scatter_dimension=1, tiled=True)
    down_part = jnp.einsum(
        "ntd,ndr->ntr", token_tiles, down_panel, preferred_element_type=jnp.float32
    )
    down_sum = lax.psum(down_part, "mp")
    down_portion = down_sum.astype(jnp.bfloat16)
    adapter_term = jnp.einsum(
        "ntr,nrv->ntv", down_portion, up_panel, preferred_element_type=jnp.float32
    ).reshape(tok_count, head_cols)
    projected = (
        (frozen_local + adapter_scale * adapter_term) * active_rows.astype(jnp.float32)
    ).astype(jnp.bfloat16)
    tile_mask = masked_own.reshape(tiles_here, TILE, head_cols)
    backward_piece = adapter_scale * jnp.einsum(
        "ntv,nrv->ntr", tile_mask, up_panel, preferred_element_type=jnp.float32
    )
    backward_portion = lax.psum(backward_piece, "mp").astype(jnp.bfloat16)
    frozen_backward = lax.dot_general(
        masked_full,
        lax.all_gather(value_weight, "adapter", axis=1, tiled=True),
        (((1,), (1,)), ((), ())),
        preferred_element_type=jnp.float32,
    )
    adapter_backward = jnp.einsum(
        "ntr,ndr->ntd", backward_portion, down_panel, preferred_element_type=jnp.float32
    ).reshape(tok_count, feat_part)
    token_gradient = (frozen_backward + adapter_backward).astype(jnp.bfloat16)
    home_down = jnp.einsum(
        "ntd,ntr->ndr", token_tiles, backward_portion, preferred_element_type=jnp.float32
    )
    local_up_weight = adapter_scale * jnp.einsum(
        "ntr,ntv->nrv", down_portion, tile_mask, preferred_element_type=jnp.float32
    )
    arrived_down, arrived_up = (
        lax.all_to_all(home_down, "adapter", split_axis=1, concat_axis=0, tiled=True),
        lax.all_to_all(local_up_weight, "adapter", split_axis=1, concat_axis=0, tiled=True),
    )
    selector = (adapter_ids[:, None] == tile_adapter_slot[None, :]).astype(jnp.float32)
    down_gradient = jnp.dot(
        selector, arrived_down.reshape(tile_total, -1), precision=lax.Precision.HIGHEST
    ).reshape(down_store.shape)
    up_gradient = jnp.dot(
        selector, arrived_up.reshape(tile_total, -1), precision=lax.Precision.HIGHEST
    ).reshape(up_store.shape)
    new_down, new_down_first, new_down_second = adam_step(
        down_store, down_first, down_second, down_gradient
    )
    new_up, new_up_first, new_up_second = adam_step(up_store, up_first, up_second, up_gradient)
    return (
        projected,
        token_gradient,
        new_down,
        new_down_first,
        new_down_second,
        new_up,
        new_up_first,
        new_up_second,
    )


F32 = jnp.float32
BF16 = jnp.bfloat16
NT = (((1,), (1,)), ((), ()))
TN = (((0,), (0,)), ((), ()))


def dot(a, b, dims=(((1,), (0,)), ((), ()))):
    return lax.dot_general(a, b, dims, preferred_element_type=F32)


def fused_kernel(
    na,
    nm,
    tad,
    tlen,
    aslot,
    tok,
    cot,
    w,
    down,
    up,
    proj,
    tgrad,
    gdown,
    gup,
    wbuf,
    masked,
    sel_d,
    sel_u,
    pan_d,
    pan_u,
    part,
    rs_in,
    db,
    term,
    fro_send,
    fro_recv,
    fro_own,
    acc,
    g_send,
    g_recv,
    gu_send,
    gu_recv,
    wr_s,
    wl_s,
    w_r,
    pd_s,
    pd_r,
    pu_s,
    pu_r,
    ms_s,
    ms_r,
    rs_s,
    rs_r,
    ag_s,
    ag_r,
    fs_s,
    fs_r,
    gd_s,
    gd_r,
    gu_s,
    gu_r,
):
    z = lax.axis_index("adapter")
    m = lax.axis_index("mp")
    cols = cot.shape[1]
    heads = w.shape[1] // cols
    tiles = tok.shape[0] // TILE
    rank = down.shape[1]
    depth = down.shape[2]
    rank_part = up.shape[1]
    slots = down.shape[0]
    block = tok.shape[0] // nm

    def other_z(d):
        return lax.rem(z + d, na)

    def other_m(d):
        return lax.rem(m + d, nm)

    def remote(src, dst, send, recv, device):
        return pltpu.make_async_remote_copy(
            src_ref=src,
            dst_ref=dst,
            send_sem=send,
            recv_sem=recv,
            device_id=device,
            device_id_type=pl.DeviceIdType.MESH,
        )

    def to_right(g):
        return remote(
            wbuf.at[g], wbuf.at[g], wr_s.at[g], w_r.at[g], {"adapter": lax.rem(z + 1, na)}
        )

    def to_left(g):
        return remote(
            wbuf.at[g], wbuf.at[g], wl_s.at[g], w_r.at[g], {"adapter": lax.rem(z + na - 1, na)}
        )

    def panel_down(src, dst, to):
        return remote(sel_d.at[to], pan_d.at[dst], pd_s.at[to], pd_r.at[src], {"adapter": to})

    def panel_up(src, dst, to):
        return remote(sel_u.at[to], pan_u.at[dst], pu_s.at[to], pu_r.at[src], {"adapter": to})

    def mask_copy(src, to):
        return remote(masked.at[src], masked.at[src], ms_s.at[to], ms_r.at[src], {"mp": to})

    def sum_copy(src, to):
        at = pl.ds(pl.multiple_of(to * block, block), block)
        return remote(part.at[at], rs_in.at[src], rs_s.at[to], rs_r.at[src], {"mp": to})

    def rows_copy(src, to):
        at = pl.ds(pl.multiple_of(src * block, block), block)
        return remote(db.at[at], db.at[at], ag_s.at[to], ag_r.at[src], {"mp": to})

    def frozen_copy(src, to):
        return remote(
            fro_send.at[to], fro_recv.at[src], fs_s.at[to], fs_r.at[src], {"mp": to}
        )

    def grad_down_copy(src, to):
        return remote(g_send.at[to], g_recv.at[src], gd_s.at[to], gd_r.at[src], {"adapter": to})

    def grad_up_copy(src, to):
        return remote(gu_send.at[to], gu_recv.at[src], gu_s.at[to], gu_r.at[src], {"adapter": to})

    slot_of = [aslot[tad[i]] for i in range(na * tiles)]
    for i in range(na * tiles):
        sel_d[i // tiles, i % tiles] = down[slot_of[i]]
        sel_u[i // tiles, i % tiles] = up[slot_of[i]]
    pan_d[z] = sel_d[z]
    pan_u[z] = sel_u[z]
    for h in range(heads):
        wbuf[z * heads + h] = w[:, h * cols : (h + 1) * cols]

    def live(n):
        row = lax.broadcasted_iota(jnp.int32, (TILE, cols), 0)
        return jnp.where(row < tlen[z * tiles + n], 1.0, 0.0)

    for n in range(tiles):
        at = slice(n * TILE, (n + 1) * TILE)
        masked[m, at] = (cot[at].astype(F32) * live(n)).astype(BF16)

    barrier = pltpu.get_barrier_semaphore()
    for d in range(1, na):
        pl.semaphore_signal(
            barrier, inc=1, device_id={"adapter": other_z(d)}, device_id_type=pl.DeviceIdType.MESH
        )
    for d in range(1, nm):
        pl.semaphore_signal(
            barrier, inc=1, device_id={"mp": other_m(d)}, device_id_type=pl.DeviceIdType.MESH
        )
    pl.semaphore_wait(barrier, na + nm - 2)

    for d in range(1, na):
        panel_up(z, z, other_z(d)).start()
    for d in range(1, na):
        panel_down(z, z, other_z(d)).start()
    for h in range(heads):

        @pl.when(z < na - 1)
        def _():
            to_right(z * heads + h).start()

        @pl.when(z > 0)
        def _():
            to_left(z * heads + h).start()

    for d in range(1, nm):
        mask_copy(m, other_m(d)).start()

    for d in range(1, na):
        panel_up(other_z(d), z, other_z(d)).wait_recv()
    for d in range(1, na):
        panel_down(other_z(d), other_z(d), other_z(d)).wait_recv()

    def up_panel(n):
        return jnp.concatenate([pan_u[j, n] for j in range(na)], axis=0)

    for n in range(tiles):
        at = slice(n * TILE, (n + 1) * TILE)
        down_part = dot(tok[at, 0:depth], pan_d[0, n], NT)
        for j in range(1, na):
            down_part += dot(tok[at, j * depth : (j + 1) * depth], pan_d[j, n], NT)
        back_part = adapter_scale * dot(masked[m, at], up_panel(n), NT)
        part[at] = jnp.concatenate([down_part, back_part], axis=1)
    for d in range(1, nm):
        sum_copy(m, other_m(d)).start()

    def forward(g):
        value = dot(tok[...], wbuf[g])

        @pl.when(g == m)
        def _():
            fro_own[...] = value

        @pl.when(g != m)
        def _():
            fro_send[g] = value.astype(BF16)
            frozen_copy(m, g).start()

    def backward(g):
        acc[...] += dot(masked[g], wbuf[g], NT)

    def own_forward(h, carry):
        forward(z * heads + h)
        return carry

    lax.fori_loop(0, heads, own_forward, 0)

    total = part[pl.ds(pl.multiple_of(m * block, block), block)]
    for d in range(1, nm):
        sum_copy(other_m(d), other_m(d)).wait_recv()
        total += rs_in[other_m(d)]
    db[pl.ds(pl.multiple_of(m * block, block), block)] = total.astype(BF16)
    for d in range(1, nm):
        rows_copy(m, other_m(d)).start()
    for d in range(1, nm):
        rows_copy(other_m(d), other_m(d)).wait_recv()

    for n in range(tiles):
        at = slice(n * TILE, (n + 1) * TILE)
        both = db[at]
        down_rows, back_rows = both[:, :rank], both[:, rank:]
        g_tile = dot(back_rows, tok[at], TN)
        gu_tile = adapter_scale * dot(down_rows, masked[m, at], TN)
        for j in range(na):
            g_send[j, n] = g_tile[:, j * depth : (j + 1) * depth].astype(BF16)
            gu_send[j, n] = gu_tile[j * rank_part : (j + 1) * rank_part]
    for d in range(1, na):
        grad_down_copy(z, other_z(d)).start()
        grad_up_copy(z, other_z(d)).start()
    g_recv[z] = g_send[z]
    gu_recv[z] = gu_send[z]
    for n in range(tiles):
        at = slice(n * TILE, (n + 1) * TILE)
        both = db[at]
        down_rows, back_rows = both[:, :rank], both[:, rank:]
        term[at] = adapter_scale * dot(down_rows, up_panel(n))
        for j in range(na):
            acc[at, j * depth : (j + 1) * depth] = dot(back_rows, pan_d[j, n])

    for d in range(1, nm):
        mask_copy(other_m(d), other_m(d)).wait_recv()

    def own_backward(h, carry):
        backward(z * heads + h)
        return carry

    lax.fori_loop(0, heads, own_backward, 0)

    def relay(t, carry):
        step = t // heads + 1
        h = lax.rem(t, heads)
        lower = (z - step) * heads + h
        upper = (z + step) * heads + h

        @pl.when(z >= step)
        def _():
            to_right(lower).wait_recv()

            @pl.when(z < na - 1)
            def _():
                to_right(lower).start()

        @pl.when(z + step < na)
        def _():
            to_left(upper).wait_recv()

            @pl.when(z > 0)
            def _():
                to_left(upper).start()

        def one(side, inner):
            head = (z + (2 * side - 1) * step) * heads + h
            valid = jnp.logical_and(head >= 0, head < na * heads)

            @pl.when(valid)
            def _():
                forward(head)
                backward(head)

            return inner

        return lax.fori_loop(0, 2, one, carry)

    lax.fori_loop(0, (na - 1) * heads, relay, 0)

    for d in range(1, na):
        grad_down_copy(other_z(d), other_z(d)).wait_recv()
        grad_up_copy(other_z(d), other_z(d)).wait_recv()

    def slot_sum(s, carry):
        total_d = jnp.zeros((rank, depth), F32)
        total_u = jnp.zeros((rank_part, cols), F32)
        for i in range(na * tiles):
            use = jnp.where(slot_of[i] == s, 1.0, 0.0)
            total_d += use * g_recv[i // tiles, i % tiles].astype(F32)
            total_u += use * gu_recv[i // tiles, i % tiles]
        gdown[s] = total_d
        gup[s] = total_u
        return carry

    lax.fori_loop(0, slots, slot_sum, 0)
    tgrad[...] = acc[...].astype(BF16)

    for d in range(1, nm):
        frozen_copy(other_m(d), other_m(d)).wait_recv()
    for n in range(tiles):
        at = slice(n * TILE, (n + 1) * TILE)
        value = fro_own[at] + term[at]
        for d in range(1, nm):
            value += fro_recv[other_m(d), at].astype(F32)
        proj[at] = (value * live(n)).astype(BF16)

    for d in range(1, na):
        panel_up(z, z, other_z(d)).wait_send()
        panel_down(z, z, other_z(d)).wait_send()
        grad_down_copy(z, other_z(d)).wait_send()
        grad_up_copy(z, other_z(d)).wait_send()
    for d in range(1, nm):
        mask_copy(m, other_m(d)).wait_send()
        sum_copy(m, other_m(d)).wait_send()
        rows_copy(m, other_m(d)).wait_send()
        frozen_copy(m, other_m(d)).wait_send()

    def drain(g, carry):
        owner = g // heads

        @pl.when(jnp.logical_and(owner <= z, z < na - 1))
        def _():
            to_right(g).wait_send()

        @pl.when(jnp.logical_and(owner >= z, z > 0))
        def _():
            to_left(g).wait_send()

        return carry

    lax.fori_loop(0, na * heads, drain, 0)


def fused_shards(
    na,
    nm,
    tokens,
    cotangent,
    value_weight,
    down_store,
    down_first,
    down_second,
    up_store,
    up_first,
    up_second,
    tile_adapter,
    tile_length,
    adapter_slot,
):
    rows, feats = tokens.shape
    cols = cotangent.shape[1]
    tiles = rows // TILE
    slots, _, depth, rank = down_store.shape
    part = up_store.shape[1]
    down_t = jnp.swapaxes(down_store[:, 0], 1, 2)
    vmem = pl.BlockSpec(memory_space=pltpu.VMEM)
    smem = pl.BlockSpec(memory_space=pltpu.SMEM)
    dma = pltpu.SemaphoreType.DMA
    sds = jax.ShapeDtypeStruct
    proj, tgrad, gdown, gup = pl.pallas_call(
        functools.partial(fused_kernel, na, nm),
        out_shape=(
            sds((rows, cols), BF16),
            sds((rows, feats), BF16),
            sds((slots, rank, depth), F32),
            sds((slots, part, cols), F32),
        ),
        in_specs=[smem] * 3 + [vmem] * 5,
        out_specs=(vmem,) * 4,
        scratch_shapes=[
            pltpu.VMEM((nm, feats, cols), BF16),
            pltpu.VMEM((nm, rows, cols), BF16),
            pltpu.VMEM((na, tiles, rank, depth), BF16),
            pltpu.VMEM((na, tiles, part, cols), BF16),
            pltpu.VMEM((na, tiles, rank, depth), BF16),
            pltpu.VMEM((na, tiles, part, cols), BF16),
            pltpu.VMEM((rows, 2 * rank), F32),
            pltpu.VMEM((nm, rows // nm, 2 * rank), F32),
            pltpu.VMEM((rows, 2 * rank), BF16),
            pltpu.VMEM((rows, cols), F32),
            pltpu.VMEM((nm, rows, cols), BF16),
            pltpu.VMEM((nm, rows, cols), BF16),
            pltpu.VMEM((rows, cols), F32),
            pltpu.VMEM((rows, feats), F32),
            pltpu.VMEM((na, tiles, rank, depth), BF16),
            pltpu.VMEM((na, tiles, rank, depth), BF16),
            pltpu.VMEM((na, tiles, part, cols), F32),
            pltpu.VMEM((na, tiles, part, cols), F32),
            dma((nm,)),
            dma((nm,)),
            dma((nm,)),
            dma((na,)),
            dma((na,)),
            dma((na,)),
            dma((na,)),
            dma((nm,)),
            dma((nm,)),
            dma((nm,)),
            dma((nm,)),
            dma((nm,)),
            dma((nm,)),
            dma((nm,)),
            dma((nm,)),
            dma((na,)),
            dma((na,)),
            dma((na,)),
            dma((na,)),
        ],
        compiler_params=pltpu.CompilerParams(
            collective_id=0, has_side_effects=True, vmem_limit_bytes=40 * 1024 * 1024
        ),
    )(tile_adapter, tile_length, adapter_slot, tokens, cotangent, value_weight, down_t, up_store)
    down_gradient = jnp.swapaxes(gdown, 1, 2)[:, None]
    return (
        proj,
        tgrad,
        *adam_step(down_store, down_first, down_second, down_gradient),
        *adam_step(up_store, up_first, up_second, gup),
    )


def by_share(na, nm, *arrays):
    rows, cols = arrays[1].shape
    share = arrays[2].shape[1]
    fits = cols % 128 == 0 and share % cols == 0 and rows % (16 * nm) == 0
    return fused_shards(na, nm, *arrays) if fits else shards(*arrays)


def solution(mesh):
    placed = (
        P("adapter", "mp"),
        P("adapter", "mp"),
        P("mp", "adapter"),
        P(None, "mp", "adapter", None),
        P(None, "mp", "adapter", None),
        P(None, "mp", "adapter", None),
        P(None, "adapter", "mp"),
        P(None, "adapter", "mp"),
        P(None, "adapter", "mp"),
        P(),
        P(),
        P(),
    )
    return jax.shard_map(
        functools.partial(by_share, mesh.shape["adapter"], mesh.shape["mp"]),
        mesh=mesh,
        in_specs=placed,
        out_specs=(
            P("adapter", "mp"),
            P("adapter", "mp"),
            P(None, "mp", "adapter", None),
            P(None, "mp", "adapter", None),
            P(None, "mp", "adapter", None),
            P(None, "adapter", "mp"),
            P(None, "adapter", "mp"),
            P(None, "adapter", "mp"),
        ),
        check_vma=False,
    )
```

```python
import functools

import jax
import jax.numpy as jnp
from jax import lax
from jax.experimental import pallas as pl
from jax.experimental.pallas import tpu as pltpu
from jax.sharding import PartitionSpec as P

TILE = 128
STEP = 100


adapter_scale = 2.0
learn_rate = 0.001
beta_one = 0.9
beta_two = 0.999
adam_eps = 1e-08


def adam_step(store, first, second, gradient):
    new_first = beta_one * first + (1.0 - beta_one) * gradient
    new_second = beta_two * second + (1.0 - beta_two) * gradient * gradient
    corr_one = 1.0 - beta_one**STEP
    corr_two = 1.0 - beta_two**STEP
    moved = store.astype(jnp.float32) - learn_rate * (new_first / corr_one) / (
        jnp.sqrt(new_second / corr_two) + adam_eps
    )
    return (moved, new_first, new_second)


def shards(
    tokens,
    cotangent,
    value_weight,
    down_store,
    down_first,
    down_second,
    up_store,
    up_first,
    up_second,
    tile_adapter,
    tile_length,
    adapter_slot,
):
    tile_total = tile_adapter.shape[0]
    tok_count, feat_part = tokens.shape
    head_cols = cotangent.shape[1]
    tiles_here = tok_count // TILE
    adapter_count = adapter_slot.shape[0]
    my_index = lax.axis_index("adapter")
    adapter_ids = jnp.arange(adapter_count, dtype=jnp.int32)
    tile_adapter_slot = jnp.sum(
        jnp.where(tile_adapter[:, None] == adapter_ids[None, :], adapter_slot[None, :], 0), axis=1
    )
    my_lengths = lax.dynamic_slice_in_dim(tile_length, my_index * tiles_here, tiles_here)
    active_rows = (jnp.arange(TILE)[None, :] < my_lengths[:, None]).reshape(tok_count, 1)
    masked_own = cotangent * active_rows.astype(jnp.bfloat16)
    masked_full = lax.all_gather(masked_own, "mp", axis=1, tiled=True)
    sent_down = down_store[:, 0][tile_adapter_slot]
    sent_up = up_store[tile_adapter_slot]
    down_panel, up_panel = (
        lax.all_to_all(sent_down, "adapter", split_axis=0, concat_axis=1, tiled=True),
        lax.all_to_all(sent_up, "adapter", split_axis=0, concat_axis=1, tiled=True),
    )
    token_tiles = tokens.reshape(tiles_here, TILE, feat_part)
    frozen_part = jnp.dot(
        tokens,
        lax.all_gather(value_weight, "adapter", axis=1, tiled=True),
        preferred_element_type=jnp.float32,
    )
    frozen_local = lax.psum_scatter(frozen_part, "mp", scatter_dimension=1, tiled=True)
    down_part = jnp.einsum(
        "ntd,ndr->ntr", token_tiles, down_panel, preferred_element_type=jnp.float32
    )
    down_sum = lax.psum(down_part, "mp")
    down_portion = down_sum.astype(jnp.bfloat16)
    adapter_term = jnp.einsum(
        "ntr,nrv->ntv", down_portion, up_panel, preferred_element_type=jnp.float32
    ).reshape(tok_count, head_cols)
    projected = (
        (frozen_local + adapter_scale * adapter_term) * active_rows.astype(jnp.float32)
    ).astype(jnp.bfloat16)
    tile_mask = masked_own.reshape(tiles_here, TILE, head_cols)
    backward_piece = adapter_scale * jnp.einsum(
        "ntv,nrv->ntr", tile_mask, up_panel, preferred_element_type=jnp.float32
    )
    backward_portion = lax.psum(backward_piece, "mp").astype(jnp.bfloat16)
    frozen_backward = lax.dot_general(
        masked_full,
        lax.all_gather(value_weight, "adapter", axis=1, tiled=True),
        (((1,), (1,)), ((), ())),
        preferred_element_type=jnp.float32,
    )
    adapter_backward = jnp.einsum(
        "ntr,ndr->ntd", backward_portion, down_panel, preferred_element_type=jnp.float32
    ).reshape(tok_count, feat_part)
    token_gradient = (frozen_backward + adapter_backward).astype(jnp.bfloat16)
    home_down = jnp.einsum(
        "ntd,ntr->ndr", token_tiles, backward_portion, preferred_element_type=jnp.float32
    )
    local_up_weight = adapter_scale * jnp.einsum(
        "ntr,ntv->nrv", down_portion, tile_mask, preferred_element_type=jnp.float32
    )
    arrived_down, arrived_up = (
        lax.all_to_all(home_down, "adapter", split_axis=1, concat_axis=0, tiled=True),
        lax.all_to_all(local_up_weight, "adapter", split_axis=1, concat_axis=0, tiled=True),
    )
    selector = (adapter_ids[:, None] == tile_adapter_slot[None, :]).astype(jnp.float32)
    down_gradient = jnp.dot(
        selector, arrived_down.reshape(tile_total, -1), precision=lax.Precision.HIGHEST
    ).reshape(down_store.shape)
    up_gradient = jnp.dot(
        selector, arrived_up.reshape(tile_total, -1), precision=lax.Precision.HIGHEST
    ).reshape(up_store.shape)
    new_down, new_down_first, new_down_second = adam_step(
        down_store, down_first, down_second, down_gradient
    )
    new_up, new_up_first, new_up_second = adam_step(up_store, up_first, up_second, up_gradient)
    return (
        projected,
        token_gradient,
        new_down,
        new_down_first,
        new_down_second,
        new_up,
        new_up_first,
        new_up_second,
    )


F32 = jnp.float32
BF16 = jnp.bfloat16
NT = (((1,), (1,)), ((), ()))
TN = (((0,), (0,)), ((), ()))


def dot(a, b, dims=(((1,), (0,)), ((), ()))):
    return lax.dot_general(a, b, dims, preferred_element_type=F32)


def fused_kernel(
    na,
    nm,
    tad,
    tlen,
    aslot,
    tok_hbm,
    cot_hbm,
    w,
    down_hbm,
    up_hbm,
    proj,
    tgrad,
    gdown,
    gup,
    tok,
    cot,
    down,
    up,
    wbuf,
    masked,
    sel_d,
    sel_u,
    pan_d,
    pan_u,
    part,
    rs_in,
    db,
    term,
    fro_send,
    fro_recv,
    fro_own,
    acc,
    g_send,
    g_recv,
    gu_send,
    gu_recv,
    wr_s,
    wl_s,
    w_r,
    pd_s,
    pd_r,
    pu_s,
    pu_r,
    ms_s,
    ms_r,
    rs_s,
    rs_r,
    ag_s,
    ag_r,
    fs_s,
    fs_r,
    gd_s,
    gd_r,
    gu_s,
    gu_r,
    load,
    w_load,
):
    z = lax.axis_index("adapter")
    m = lax.axis_index("mp")
    cols = cot.shape[1]
    heads = w.shape[1] // cols
    tiles = tok.shape[0] // TILE
    rank = down.shape[1]
    depth = down.shape[2]
    rank_part = up.shape[1]
    slots = down.shape[0]
    block = tok.shape[0] // nm

    def other_z(d):
        return lax.rem(z + d, na)

    def other_m(d):
        return lax.rem(m + d, nm)

    def remote(src, dst, send, recv, device):
        return pltpu.make_async_remote_copy(
            src_ref=src,
            dst_ref=dst,
            send_sem=send,
            recv_sem=recv,
            device_id=device,
            device_id_type=pl.DeviceIdType.MESH,
        )

    def to_right(g):
        return remote(
            wbuf.at[g], wbuf.at[g], wr_s.at[g], w_r.at[g], {"adapter": lax.rem(z + 1, na)}
        )

    def to_left(g):
        return remote(
            wbuf.at[g], wbuf.at[g], wl_s.at[g], w_r.at[g], {"adapter": lax.rem(z + na - 1, na)}
        )

    def panel_down(src, dst, to):
        return remote(sel_d.at[to], pan_d.at[dst], pd_s.at[to], pd_r.at[src], {"adapter": to})

    def panel_up(src, dst, to):
        return remote(sel_u.at[to], pan_u.at[dst], pu_s.at[to], pu_r.at[src], {"adapter": to})

    def mask_copy(src, to):
        return remote(masked.at[src], masked.at[src], ms_s.at[to], ms_r.at[src], {"mp": to})

    def sum_copy(src, to):
        at = pl.ds(pl.multiple_of(to * block, block), block)
        return remote(part.at[at], rs_in.at[src], rs_s.at[to], rs_r.at[src], {"mp": to})

    def rows_copy(src, to):
        at = pl.ds(pl.multiple_of(src * block, block), block)
        return remote(db.at[at], db.at[at], ag_s.at[to], ag_r.at[src], {"mp": to})

    def frozen_copy(src, to):
        return remote(
            fro_send.at[to], fro_recv.at[src], fs_s.at[to], fs_r.at[src], {"mp": to}
        )

    def grad_down_copy(src, to):
        return remote(g_send.at[to], g_recv.at[src], gd_s.at[to], gd_r.at[src], {"adapter": to})

    def grad_up_copy(src, to):
        return remote(gu_send.at[to], gu_recv.at[src], gu_s.at[to], gu_r.at[src], {"adapter": to})

    loads = [
        pltpu.make_async_copy(src, dst, load.at[i])
        for i, (src, dst) in enumerate(
            ((down_hbm, down), (up_hbm, up), (cot_hbm, cot), (tok_hbm, tok))
        )
    ]
    w_loads = [
        pltpu.make_async_copy(
            w.at[:, pl.ds(h * cols, cols)], wbuf.at[z * heads + h], w_load.at[h]
        )
        for h in range(heads)
    ]
    barrier = pltpu.get_barrier_semaphore()
    for d in range(1, na):
        pl.semaphore_signal(
            barrier, inc=1, device_id={"adapter": other_z(d)}, device_id_type=pl.DeviceIdType.MESH
        )
    for d in range(1, nm):
        pl.semaphore_signal(
            barrier, inc=1, device_id={"mp": other_m(d)}, device_id_type=pl.DeviceIdType.MESH
        )
    for copy in w_loads + loads:
        copy.start()

    slot_of = [aslot[tad[i]] for i in range(na * tiles)]

    def live(n):
        row = lax.broadcasted_iota(jnp.int32, (TILE, cols), 0)
        return jnp.where(row < tlen[z * tiles + n], 1.0, 0.0)

    def send_own(h):
        @pl.when(z < na - 1)
        def _():
            to_right(z * heads + h).start()

        @pl.when(z > 0)
        def _():
            to_left(z * heads + h).start()

    loads[0].wait()
    loads[1].wait()
    for i in range(na * tiles):
        sel_d[i // tiles, i % tiles] = down[slot_of[i]]
        sel_u[i // tiles, i % tiles] = up[slot_of[i]]
    loads[2].wait()
    for n in range(tiles):
        at = slice(n * TILE, (n + 1) * TILE)
        masked[m, at] = (cot[at].astype(F32) * live(n)).astype(BF16)
    for copy in w_loads:
        copy.wait()
    pl.semaphore_wait(barrier, na + nm - 2)

    send_own(0)
    for d in range(1, na):
        panel_up(z, z, other_z(d)).start()
    for d in range(1, na):
        panel_down(z, z, other_z(d)).start()
    for h in range(1, heads):
        send_own(h)
    for d in range(1, nm):
        mask_copy(m, other_m(d)).start()
    pan_d[z] = sel_d[z]
    pan_u[z] = sel_u[z]
    loads[3].wait()

    def forward(g):
        value = dot(tok[...], wbuf[g])

        @pl.when(g == m)
        def _():
            fro_own[...] = value

        @pl.when(g != m)
        def _():
            fro_send[g] = value.astype(BF16)
            frozen_copy(m, g).start()

    def backward(g):
        acc[...] += dot(masked[g], wbuf[g], NT)

    def own_forward(h, carry):
        forward(z * heads + h)
        return carry

    def own_backward(h, carry):
        backward(z * heads + h)
        return carry

    def pass_on(t):
        step = t // heads + 1
        h = lax.rem(t, heads)
        lower = (z - step) * heads + h
        upper = (z + step) * heads + h

        @pl.when(z >= step)
        def _():
            to_right(lower).wait_recv()

            @pl.when(z < na - 1)
            def _():
                to_right(lower).start()

        @pl.when(z + step < na)
        def _():
            to_left(upper).wait_recv()

            @pl.when(z > 0)
            def _():
                to_left(upper).start()

    def multiply(t):
        step = t // heads + 1
        h = lax.rem(t, heads)

        def one(side, inner):
            head = (z + (2 * lax.rem(side, 2) - 1) * step) * heads + h
            valid = jnp.logical_and(head >= 0, head < na * heads)

            @pl.when(jnp.logical_and(valid, side < 2))
            def _():
                forward(head)

            @pl.when(jnp.logical_and(valid, side >= 2))
            def _():
                backward(head)

            return inner

        lax.fori_loop(0, 4, one, 0)

    lax.fori_loop(0, heads, own_forward, 0)

    for d in range(1, na):
        panel_up(other_z(d), z, other_z(d)).wait_recv()
    for d in range(1, na):
        panel_down(other_z(d), other_z(d), other_z(d)).wait_recv()

    def up_panel(n):
        return jnp.concatenate([pan_u[j, n] for j in range(na)], axis=0)

    for n in range(tiles):
        at = slice(n * TILE, (n + 1) * TILE)
        down_part = dot(tok[at, 0:depth], pan_d[0, n], NT)
        for j in range(1, na):
            down_part += dot(tok[at, j * depth : (j + 1) * depth], pan_d[j, n], NT)
        back_part = adapter_scale * dot(masked[m, at], up_panel(n), NT)
        part[at] = jnp.concatenate([down_part, back_part], axis=1)
    for d in range(1, nm):
        sum_copy(m, other_m(d)).start()

    pass_on(0)

    total = part[pl.ds(pl.multiple_of(m * block, block), block)]
    for d in range(1, nm):
        sum_copy(other_m(d), other_m(d)).wait_recv()
        total += rs_in[other_m(d)]
    db[pl.ds(pl.multiple_of(m * block, block), block)] = total.astype(BF16)
    for d in range(1, nm):
        rows_copy(m, other_m(d)).start()

    for d in range(1, nm):
        mask_copy(other_m(d), other_m(d)).wait_recv()
    acc[...] = jnp.zeros_like(acc)
    lax.fori_loop(0, heads, own_backward, 0)
    for d in range(1, nm):
        rows_copy(other_m(d), other_m(d)).wait_recv()

    for n in range(tiles):
        at = slice(n * TILE, (n + 1) * TILE)
        both = db[at]
        down_rows, back_rows = both[:, :rank], both[:, rank:]
        g_tile = dot(back_rows, tok[at], TN)
        gu_tile = adapter_scale * dot(down_rows, masked[m, at], TN)
        for j in range(na):
            g_send[j, n] = g_tile[:, j * depth : (j + 1) * depth].astype(BF16)
            gu_send[j, n] = gu_tile[j * rank_part : (j + 1) * rank_part]
    for d in range(1, na):
        grad_down_copy(z, other_z(d)).start()
        grad_up_copy(z, other_z(d)).start()
    if heads > 1:
        pass_on(1)
    g_recv[z] = g_send[z]
    gu_recv[z] = gu_send[z]
    for n in range(tiles):
        at = slice(n * TILE, (n + 1) * TILE)
        both = db[at]
        down_rows, back_rows = both[:, :rank], both[:, rank:]
        term[at] = adapter_scale * dot(down_rows, up_panel(n))
        for j in range(na):
            acc[at, j * depth : (j + 1) * depth] += dot(back_rows, pan_d[j, n])

    early = min(heads, 2)

    def relay(t, carry):
        @pl.when(t >= early)
        def _():
            pass_on(t)

        multiply(t)
        return carry

    lax.fori_loop(0, (na - 1) * heads, relay, 0)

    for d in range(1, na):
        grad_down_copy(other_z(d), other_z(d)).wait_recv()
        grad_up_copy(other_z(d), other_z(d)).wait_recv()

    def slot_sum(s, carry):
        total_d = jnp.zeros((rank, depth), F32)
        total_u = jnp.zeros((rank_part, cols), F32)
        for i in range(na * tiles):
            use = jnp.where(slot_of[i] == s, 1.0, 0.0)
            total_d += use * g_recv[i // tiles, i % tiles].astype(F32)
            total_u += use * gu_recv[i // tiles, i % tiles]
        gdown[s] = total_d
        gup[s] = total_u
        return carry

    lax.fori_loop(0, slots, slot_sum, 0)
    tgrad[...] = acc[...].astype(BF16)

    for d in range(1, nm):
        frozen_copy(other_m(d), other_m(d)).wait_recv()
    for n in range(tiles):
        at = slice(n * TILE, (n + 1) * TILE)
        value = fro_own[at] + term[at]
        for d in range(1, nm):
            value += fro_recv[other_m(d), at].astype(F32)
        proj[at] = (value * live(n)).astype(BF16)

    for d in range(1, na):
        panel_up(z, z, other_z(d)).wait_send()
        panel_down(z, z, other_z(d)).wait_send()
        grad_down_copy(z, other_z(d)).wait_send()
        grad_up_copy(z, other_z(d)).wait_send()
    for d in range(1, nm):
        mask_copy(m, other_m(d)).wait_send()
        sum_copy(m, other_m(d)).wait_send()
        rows_copy(m, other_m(d)).wait_send()
        frozen_copy(m, other_m(d)).wait_send()

    def drain(g, carry):
        owner = g // heads

        @pl.when(jnp.logical_and(owner <= z, z < na - 1))
        def _():
            to_right(g).wait_send()

        @pl.when(jnp.logical_and(owner >= z, z > 0))
        def _():
            to_left(g).wait_send()

        return carry

    lax.fori_loop(0, na * heads, drain, 0)


def fused_shards(
    na,
    nm,
    tokens,
    cotangent,
    value_weight,
    down_store,
    down_first,
    down_second,
    up_store,
    up_first,
    up_second,
    tile_adapter,
    tile_length,
    adapter_slot,
):
    rows, feats = tokens.shape
    cols = cotangent.shape[1]
    tiles = rows // TILE
    slots, _, depth, rank = down_store.shape
    part = up_store.shape[1]
    down_t = jnp.swapaxes(down_store[:, 0], 1, 2)
    vmem = pl.BlockSpec(memory_space=pltpu.VMEM)
    hbm = pl.BlockSpec(memory_space=pltpu.HBM)
    smem = pl.BlockSpec(memory_space=pltpu.SMEM)
    dma = pltpu.SemaphoreType.DMA
    sds = jax.ShapeDtypeStruct
    proj, tgrad, gdown, gup = pl.pallas_call(
        functools.partial(fused_kernel, na, nm),
        out_shape=(
            sds((rows, cols), BF16),
            sds((rows, feats), BF16),
            sds((slots, rank, depth), F32),
            sds((slots, part, cols), F32),
        ),
        in_specs=[smem] * 3 + [hbm] * 5,
        out_specs=(vmem,) * 4,
        scratch_shapes=[
            pltpu.VMEM((rows, feats), BF16),
            pltpu.VMEM((rows, cols), BF16),
            pltpu.VMEM((slots, rank, depth), BF16),
            pltpu.VMEM((slots, part, cols), BF16),
            pltpu.VMEM((nm, feats, cols), BF16),
            pltpu.VMEM((nm, rows, cols), BF16),
            pltpu.VMEM((na, tiles, rank, depth), BF16),
            pltpu.VMEM((na, tiles, part, cols), BF16),
            pltpu.VMEM((na, tiles, rank, depth), BF16),
            pltpu.VMEM((na, tiles, part, cols), BF16),
            pltpu.VMEM((rows, 2 * rank), F32),
            pltpu.VMEM((nm, rows // nm, 2 * rank), F32),
            pltpu.VMEM((rows, 2 * rank), BF16),
            pltpu.VMEM((rows, cols), F32),
            pltpu.VMEM((nm, rows, cols), BF16),
            pltpu.VMEM((nm, rows, cols), BF16),
            pltpu.VMEM((rows, cols), F32),
            pltpu.VMEM((rows, feats), F32),
            pltpu.VMEM((na, tiles, rank, depth), BF16),
            pltpu.VMEM((na, tiles, rank, depth), BF16),
            pltpu.VMEM((na, tiles, part, cols), F32),
            pltpu.VMEM((na, tiles, part, cols), F32),
            dma((nm,)),
            dma((nm,)),
            dma((nm,)),
            dma((na,)),
            dma((na,)),
            dma((na,)),
            dma((na,)),
            dma((nm,)),
            dma((nm,)),
            dma((nm,)),
            dma((nm,)),
            dma((nm,)),
            dma((nm,)),
            dma((nm,)),
            dma((nm,)),
            dma((na,)),
            dma((na,)),
            dma((na,)),
            dma((na,)),
            dma((4,)),
            dma((value_weight.shape[1] // cols,)),
        ],
        compiler_params=pltpu.CompilerParams(
            collective_id=0, has_side_effects=True, vmem_limit_bytes=56 * 1024 * 1024
        ),
    )(tile_adapter, tile_length, adapter_slot, tokens, cotangent, value_weight, down_t, up_store)
    down_gradient = jnp.swapaxes(gdown, 1, 2)[:, None]
    return (
        proj,
        tgrad,
        *adam_step(down_store, down_first, down_second, down_gradient),
        *adam_step(up_store, up_first, up_second, gup),
    )


def by_share(na, nm, *arrays):
    rows, cols = arrays[1].shape
    share = arrays[2].shape[1]
    fits = cols % 128 == 0 and share % cols == 0 and rows % (16 * nm) == 0
    return fused_shards(na, nm, *arrays) if fits else shards(*arrays)


def solution(mesh):
    placed = (
        P("adapter", "mp"),
        P("adapter", "mp"),
        P("mp", "adapter"),
        P(None, "mp", "adapter", None),
        P(None, "mp", "adapter", None),
        P(None, "mp", "adapter", None),
        P(None, "adapter", "mp"),
        P(None, "adapter", "mp"),
        P(None, "adapter", "mp"),
        P(),
        P(),
        P(),
    )
    return jax.shard_map(
        functools.partial(by_share, mesh.shape["adapter"], mesh.shape["mp"]),
        mesh=mesh,
        in_specs=placed,
        out_specs=(
            P("adapter", "mp"),
            P("adapter", "mp"),
            P(None, "mp", "adapter", None),
            P(None, "mp", "adapter", None),
            P(None, "mp", "adapter", None),
            P(None, "adapter", "mp"),
            P(None, "adapter", "mp"),
            P(None, "adapter", "mp"),
        ),
        check_vma=False,
    )
```

```python
import functools

import jax
import jax.numpy as jnp
from jax import lax
from jax.experimental import pallas as pl
from jax.experimental.pallas import tpu as pltpu
from jax.sharding import PartitionSpec as P

TILE = 128
STEP = 100


adapter_scale = 2.0
learn_rate = 0.001
beta_one = 0.9
beta_two = 0.999
adam_eps = 1e-08


def adam_step(store, first, second, gradient):
    new_first = beta_one * first + (1.0 - beta_one) * gradient
    new_second = beta_two * second + (1.0 - beta_two) * gradient * gradient
    corr_one = 1.0 - beta_one**STEP
    corr_two = 1.0 - beta_two**STEP
    moved = store.astype(jnp.float32) - learn_rate * (new_first / corr_one) / (
        jnp.sqrt(new_second / corr_two) + adam_eps
    )
    return (moved, new_first, new_second)


def shards(
    tokens,
    cotangent,
    value_weight,
    down_store,
    down_first,
    down_second,
    up_store,
    up_first,
    up_second,
    tile_adapter,
    tile_length,
    adapter_slot,
):
    tile_total = tile_adapter.shape[0]
    tok_count, feat_part = tokens.shape
    head_cols = cotangent.shape[1]
    tiles_here = tok_count // TILE
    adapter_count = adapter_slot.shape[0]
    my_index = lax.axis_index("adapter")
    adapter_ids = jnp.arange(adapter_count, dtype=jnp.int32)
    tile_adapter_slot = jnp.sum(
        jnp.where(tile_adapter[:, None] == adapter_ids[None, :], adapter_slot[None, :], 0), axis=1
    )
    my_lengths = lax.dynamic_slice_in_dim(tile_length, my_index * tiles_here, tiles_here)
    active_rows = (jnp.arange(TILE)[None, :] < my_lengths[:, None]).reshape(tok_count, 1)
    masked_own = cotangent * active_rows.astype(jnp.bfloat16)
    masked_full = lax.all_gather(masked_own, "mp", axis=1, tiled=True)
    sent_down = down_store[:, 0][tile_adapter_slot]
    sent_up = up_store[tile_adapter_slot]
    down_panel, up_panel = (
        lax.all_to_all(sent_down, "adapter", split_axis=0, concat_axis=1, tiled=True),
        lax.all_to_all(sent_up, "adapter", split_axis=0, concat_axis=1, tiled=True),
    )
    token_tiles = tokens.reshape(tiles_here, TILE, feat_part)
    frozen_part = jnp.dot(
        tokens,
        lax.all_gather(value_weight, "adapter", axis=1, tiled=True),
        preferred_element_type=jnp.float32,
    )
    frozen_local = lax.psum_scatter(frozen_part, "mp", scatter_dimension=1, tiled=True)
    down_part = jnp.einsum(
        "ntd,ndr->ntr", token_tiles, down_panel, preferred_element_type=jnp.float32
    )
    down_sum = lax.psum(down_part, "mp")
    down_portion = down_sum.astype(jnp.bfloat16)
    adapter_term = jnp.einsum(
        "ntr,nrv->ntv", down_portion, up_panel, preferred_element_type=jnp.float32
    ).reshape(tok_count, head_cols)
    projected = (
        (frozen_local + adapter_scale * adapter_term) * active_rows.astype(jnp.float32)
    ).astype(jnp.bfloat16)
    tile_mask = masked_own.reshape(tiles_here, TILE, head_cols)
    backward_piece = adapter_scale * jnp.einsum(
        "ntv,nrv->ntr", tile_mask, up_panel, preferred_element_type=jnp.float32
    )
    backward_portion = lax.psum(backward_piece, "mp").astype(jnp.bfloat16)
    frozen_backward = lax.dot_general(
        masked_full,
        lax.all_gather(value_weight, "adapter", axis=1, tiled=True),
        (((1,), (1,)), ((), ())),
        preferred_element_type=jnp.float32,
    )
    adapter_backward = jnp.einsum(
        "ntr,ndr->ntd", backward_portion, down_panel, preferred_element_type=jnp.float32
    ).reshape(tok_count, feat_part)
    token_gradient = (frozen_backward + adapter_backward).astype(jnp.bfloat16)
    home_down = jnp.einsum(
        "ntd,ntr->ndr", token_tiles, backward_portion, preferred_element_type=jnp.float32
    )
    local_up_weight = adapter_scale * jnp.einsum(
        "ntr,ntv->nrv", down_portion, tile_mask, preferred_element_type=jnp.float32
    )
    arrived_down, arrived_up = (
        lax.all_to_all(home_down, "adapter", split_axis=1, concat_axis=0, tiled=True),
        lax.all_to_all(local_up_weight, "adapter", split_axis=1, concat_axis=0, tiled=True),
    )
    selector = (adapter_ids[:, None] == tile_adapter_slot[None, :]).astype(jnp.float32)
    down_gradient = jnp.dot(
        selector, arrived_down.reshape(tile_total, -1), precision=lax.Precision.HIGHEST
    ).reshape(down_store.shape)
    up_gradient = jnp.dot(
        selector, arrived_up.reshape(tile_total, -1), precision=lax.Precision.HIGHEST
    ).reshape(up_store.shape)
    new_down, new_down_first, new_down_second = adam_step(
        down_store, down_first, down_second, down_gradient
    )
    new_up, new_up_first, new_up_second = adam_step(up_store, up_first, up_second, up_gradient)
    return (
        projected,
        token_gradient,
        new_down,
        new_down_first,
        new_down_second,
        new_up,
        new_up_first,
        new_up_second,
    )


F32 = jnp.float32
BF16 = jnp.bfloat16
NT = (((1,), (1,)), ((), ()))
TN = (((0,), (0,)), ((), ()))


def dot(a, b, dims=(((1,), (0,)), ((), ()))):
    return lax.dot_general(a, b, dims, preferred_element_type=F32)


def fused_kernel(
    na,
    nm,
    tad,
    tlen,
    aslot,
    tok_hbm,
    cot_hbm,
    w,
    down_hbm,
    up_hbm,
    proj,
    tgrad,
    gdown,
    gup,
    tok,
    cot,
    down,
    up,
    wbuf,
    masked,
    sel_d,
    sel_u,
    pan_d,
    pan_u,
    part,
    rs_in,
    db,
    term,
    fro_send,
    fro_recv,
    fro_own,
    acc,
    g_send,
    g_recv,
    gu_send,
    gu_recv,
    wr_s,
    wl_s,
    w_r,
    pd_s,
    pd_r,
    pu_s,
    pu_r,
    ms_s,
    ms_r,
    rs_s,
    rs_r,
    ag_s,
    ag_r,
    fs_s,
    fs_r,
    gd_s,
    gd_r,
    gu_s,
    gu_r,
    load,
    w_load,
):
    z = lax.axis_index("adapter")
    m = lax.axis_index("mp")
    cols = cot.shape[1]
    heads = w.shape[1] // cols
    tiles = tok.shape[0] // TILE
    rank = down.shape[1]
    depth = down.shape[2]
    rank_part = up.shape[1]
    slots = down.shape[0]
    block = tok.shape[0] // nm

    def other_z(d):
        return lax.rem(z + d, na)

    def other_m(d):
        return lax.rem(m + d, nm)

    def remote(src, dst, send, recv, device):
        return pltpu.make_async_remote_copy(
            src_ref=src,
            dst_ref=dst,
            send_sem=send,
            recv_sem=recv,
            device_id=device,
            device_id_type=pl.DeviceIdType.MESH,
        )

    def to_right(g):
        return remote(
            wbuf.at[g], wbuf.at[g], wr_s.at[g], w_r.at[g], {"adapter": lax.rem(z + 1, na)}
        )

    def to_left(g):
        return remote(
            wbuf.at[g], wbuf.at[g], wl_s.at[g], w_r.at[g], {"adapter": lax.rem(z + na - 1, na)}
        )

    def panel_down(src, dst, to):
        return remote(sel_d.at[to], pan_d.at[dst], pd_s.at[to], pd_r.at[src], {"adapter": to})

    def panel_up(src, dst, to):
        return remote(sel_u.at[to], pan_u.at[dst], pu_s.at[to], pu_r.at[src], {"adapter": to})

    def mask_copy(src, to):
        return remote(masked.at[src], masked.at[src], ms_s.at[to], ms_r.at[src], {"mp": to})

    def sum_copy(src, to):
        at = pl.ds(pl.multiple_of(to * block, block), block)
        return remote(part.at[at], rs_in.at[src], rs_s.at[to], rs_r.at[src], {"mp": to})

    def rows_copy(src, to):
        at = pl.ds(pl.multiple_of(src * block, block), block)
        return remote(db.at[at], db.at[at], ag_s.at[to], ag_r.at[src], {"mp": to})

    def frozen_copy(src, to):
        return remote(
            fro_send.at[to], fro_recv.at[src], fs_s.at[to], fs_r.at[src], {"mp": to}
        )

    def grad_down_copy(src, to):
        return remote(g_send.at[to], g_recv.at[src], gd_s.at[to], gd_r.at[src], {"adapter": to})

    def grad_up_copy(src, to):
        return remote(gu_send.at[to], gu_recv.at[src], gu_s.at[to], gu_r.at[src], {"adapter": to})

    loads = [
        pltpu.make_async_copy(src, dst, load.at[i])
        for i, (src, dst) in enumerate(
            ((down_hbm, down), (up_hbm, up), (cot_hbm, cot), (tok_hbm, tok))
        )
    ]
    w_loads = [
        pltpu.make_async_copy(
            w.at[:, pl.ds(h * cols, cols)], wbuf.at[z * heads + h], w_load.at[h]
        )
        for h in range(heads)
    ]
    barrier = pltpu.get_barrier_semaphore()
    for d in range(1, na):
        pl.semaphore_signal(
            barrier, inc=1, device_id={"adapter": other_z(d)}, device_id_type=pl.DeviceIdType.MESH
        )
    for d in range(1, nm):
        pl.semaphore_signal(
            barrier, inc=1, device_id={"mp": other_m(d)}, device_id_type=pl.DeviceIdType.MESH
        )
    for copy in w_loads + loads:
        copy.start()

    slot_of = [aslot[tad[i]] for i in range(na * tiles)]

    def live(n):
        row = lax.broadcasted_iota(jnp.int32, (TILE, cols), 0)
        return jnp.where(row < tlen[z * tiles + n], 1.0, 0.0)

    def send_own(h):
        @pl.when(z < na - 1)
        def _():
            to_right(z * heads + h).start()

        @pl.when(z > 0)
        def _():
            to_left(z * heads + h).start()

    for copy in w_loads:
        copy.wait()
    pl.semaphore_wait(barrier, na + nm - 2)
    send_own(0)

    loads[0].wait()
    loads[1].wait()
    for i in range(na * tiles):
        sel_d[i // tiles, i % tiles] = down[slot_of[i]]
        sel_u[i // tiles, i % tiles] = up[slot_of[i]]
    for d in range(1, na):
        panel_up(z, z, other_z(d)).start()
    for d in range(1, na):
        panel_down(z, z, other_z(d)).start()
    for h in range(1, heads):
        send_own(h)
    loads[2].wait()
    for n in range(tiles):
        at = slice(n * TILE, (n + 1) * TILE)
        masked[m, at] = (cot[at].astype(F32) * live(n)).astype(BF16)
    for d in range(1, nm):
        mask_copy(m, other_m(d)).start()
    pan_d[z] = sel_d[z]
    pan_u[z] = sel_u[z]
    loads[3].wait()

    def forward(g):
        value = dot(tok[...], wbuf[g])

        @pl.when(g == m)
        def _():
            fro_own[...] = value

        @pl.when(g != m)
        def _():
            fro_send[g] = value.astype(BF16)
            frozen_copy(m, g).start()

    def backward(g):
        acc[...] += dot(masked[g], wbuf[g], NT)

    def own_forward(h, carry):
        forward(z * heads + h)
        return carry

    def own_backward(h, carry):
        backward(z * heads + h)
        return carry

    def pass_on(t):
        step = t // heads + 1
        h = lax.rem(t, heads)
        lower = (z - step) * heads + h
        upper = (z + step) * heads + h

        @pl.when(z >= step)
        def _():
            to_right(lower).wait_recv()

            @pl.when(z < na - 1)
            def _():
                to_right(lower).start()

        @pl.when(z + step < na)
        def _():
            to_left(upper).wait_recv()

            @pl.when(z > 0)
            def _():
                to_left(upper).start()

    def multiply(t):
        step = t // heads + 1
        h = lax.rem(t, heads)

        def one(side, inner):
            head = (z + (2 * lax.rem(side, 2) - 1) * step) * heads + h
            valid = jnp.logical_and(head >= 0, head < na * heads)

            @pl.when(jnp.logical_and(valid, side < 2))
            def _():
                forward(head)

            @pl.when(jnp.logical_and(valid, side >= 2))
            def _():
                backward(head)

            return inner

        lax.fori_loop(0, 4, one, 0)

    lax.fori_loop(0, heads, own_forward, 0)
    pass_on(0)

    for d in range(1, na):
        panel_up(other_z(d), z, other_z(d)).wait_recv()
    for d in range(1, na):
        panel_down(other_z(d), other_z(d), other_z(d)).wait_recv()

    def up_panel(n):
        return jnp.concatenate([pan_u[j, n] for j in range(na)], axis=0)

    for n in range(tiles):
        at = slice(n * TILE, (n + 1) * TILE)
        down_part = dot(tok[at, 0:depth], pan_d[0, n], NT)
        for j in range(1, na):
            down_part += dot(tok[at, j * depth : (j + 1) * depth], pan_d[j, n], NT)
        back_part = adapter_scale * dot(masked[m, at], up_panel(n), NT)
        part[at] = jnp.concatenate([down_part, back_part], axis=1)
    for d in range(1, nm):
        sum_copy(m, other_m(d)).start()

    total = part[pl.ds(pl.multiple_of(m * block, block), block)]
    for d in range(1, nm):
        sum_copy(other_m(d), other_m(d)).wait_recv()
        total += rs_in[other_m(d)]
    db[pl.ds(pl.multiple_of(m * block, block), block)] = total.astype(BF16)
    for d in range(1, nm):
        rows_copy(m, other_m(d)).start()

    for d in range(1, nm):
        mask_copy(other_m(d), other_m(d)).wait_recv()
    acc[...] = jnp.zeros_like(acc)
    lax.fori_loop(0, heads, own_backward, 0)
    for d in range(1, nm):
        rows_copy(other_m(d), other_m(d)).wait_recv()

    for n in range(tiles):
        at = slice(n * TILE, (n + 1) * TILE)
        both = db[at]
        down_rows, back_rows = both[:, :rank], both[:, rank:]
        g_tile = dot(back_rows, tok[at], TN)
        gu_tile = adapter_scale * dot(down_rows, masked[m, at], TN)
        for j in range(na):
            g_send[j, n] = g_tile[:, j * depth : (j + 1) * depth].astype(BF16)
            gu_send[j, n] = gu_tile[j * rank_part : (j + 1) * rank_part]
    for d in range(1, na):
        grad_down_copy(z, other_z(d)).start()
        grad_up_copy(z, other_z(d)).start()
    if heads > 1:
        pass_on(1)
    g_recv[z] = g_send[z]
    gu_recv[z] = gu_send[z]
    for n in range(tiles):
        at = slice(n * TILE, (n + 1) * TILE)
        both = db[at]
        down_rows, back_rows = both[:, :rank], both[:, rank:]
        term[at] = adapter_scale * dot(down_rows, up_panel(n))
        for j in range(na):
            acc[at, j * depth : (j + 1) * depth] += dot(back_rows, pan_d[j, n])

    def sum_slots():
        for d in range(1, na):
            grad_down_copy(other_z(d), other_z(d)).wait_recv()
            grad_up_copy(other_z(d), other_z(d)).wait_recv()

        def slot_sum(s, inner):
            total_d = jnp.zeros((rank, depth), F32)
            total_u = jnp.zeros((rank_part, cols), F32)
            for i in range(na * tiles):
                use = jnp.where(slot_of[i] == s, 1.0, 0.0)
                total_d += use * g_recv[i // tiles, i % tiles].astype(F32)
                total_u += use * gu_recv[i // tiles, i % tiles]
            gdown[s] = total_d
            gup[s] = total_u
            return inner

        lax.fori_loop(0, slots, slot_sum, 0)

    early = min(heads, 2)

    def relay(t, carry):
        @pl.when(t >= early)
        def _():
            pass_on(t)

        multiply(t)
        return carry

    lax.fori_loop(0, (na - 1) * heads - 1, relay, 0)
    sum_slots()
    lax.fori_loop((na - 1) * heads - 1, (na - 1) * heads, relay, 0)

    tgrad[...] = acc[...].astype(BF16)

    for d in range(1, nm):
        frozen_copy(other_m(d), other_m(d)).wait_recv()
    for n in range(tiles):
        at = slice(n * TILE, (n + 1) * TILE)
        value = fro_own[at] + term[at]
        for d in range(1, nm):
            value += fro_recv[other_m(d), at].astype(F32)
        proj[at] = (value * live(n)).astype(BF16)

    for d in range(1, na):
        panel_up(z, z, other_z(d)).wait_send()
        panel_down(z, z, other_z(d)).wait_send()
        grad_down_copy(z, other_z(d)).wait_send()
        grad_up_copy(z, other_z(d)).wait_send()
    for d in range(1, nm):
        mask_copy(m, other_m(d)).wait_send()
        sum_copy(m, other_m(d)).wait_send()
        rows_copy(m, other_m(d)).wait_send()
        frozen_copy(m, other_m(d)).wait_send()

    def drain(g, carry):
        owner = g // heads

        @pl.when(jnp.logical_and(owner <= z, z < na - 1))
        def _():
            to_right(g).wait_send()

        @pl.when(jnp.logical_and(owner >= z, z > 0))
        def _():
            to_left(g).wait_send()

        return carry

    lax.fori_loop(0, na * heads, drain, 0)


def finish_kernel(proj, tgrad, gdown, gup, down, df, dsec, up, uf, us, *outs):
    outs[0][...] = proj[...]
    outs[1][...] = tgrad[...]
    for i, (store, first, second, grad) in enumerate(
        ((down, df, dsec, gdown), (up, uf, us, gup))
    ):
        for s in range(store.shape[0]):
            values = adam_step(store[s], first[s], second[s], grad[s])
            for k, value in enumerate(values):
                outs[2 + 3 * i + k][s] = value


def fused_shards(
    na,
    nm,
    tokens,
    cotangent,
    value_weight,
    down_store,
    down_first,
    down_second,
    up_store,
    up_first,
    up_second,
    tile_adapter,
    tile_length,
    adapter_slot,
):
    rows, feats = tokens.shape
    cols = cotangent.shape[1]
    tiles = rows // TILE
    slots, _, depth, rank = down_store.shape
    part = up_store.shape[1]
    down_t = jnp.swapaxes(down_store[:, 0], 1, 2)
    vmem = pl.BlockSpec(memory_space=pltpu.VMEM)
    hbm = pl.BlockSpec(memory_space=pltpu.HBM)
    smem = pl.BlockSpec(memory_space=pltpu.SMEM)
    dma = pltpu.SemaphoreType.DMA
    sds = jax.ShapeDtypeStruct
    proj, tgrad, gdown, gup = pl.pallas_call(
        functools.partial(fused_kernel, na, nm),
        out_shape=(
            sds((rows, cols), BF16),
            sds((rows, feats), BF16),
            sds((slots, rank, depth), F32),
            sds((slots, part, cols), F32),
        ),
        in_specs=[smem] * 3 + [hbm] * 5,
        out_specs=(vmem,) * 4,
        scratch_shapes=[
            pltpu.VMEM((rows, feats), BF16),
            pltpu.VMEM((rows, cols), BF16),
            pltpu.VMEM((slots, rank, depth), BF16),
            pltpu.VMEM((slots, part, cols), BF16),
            pltpu.VMEM((nm, feats, cols), BF16),
            pltpu.VMEM((nm, rows, cols), BF16),
            pltpu.VMEM((na, tiles, rank, depth), BF16),
            pltpu.VMEM((na, tiles, part, cols), BF16),
            pltpu.VMEM((na, tiles, rank, depth), BF16),
            pltpu.VMEM((na, tiles, part, cols), BF16),
            pltpu.VMEM((rows, 2 * rank), F32),
            pltpu.VMEM((nm, rows // nm, 2 * rank), F32),
            pltpu.VMEM((rows, 2 * rank), BF16),
            pltpu.VMEM((rows, cols), F32),
            pltpu.VMEM((nm, rows, cols), BF16),
            pltpu.VMEM((nm, rows, cols), BF16),
            pltpu.VMEM((rows, cols), F32),
            pltpu.VMEM((rows, feats), F32),
            pltpu.VMEM((na, tiles, rank, depth), BF16),
            pltpu.VMEM((na, tiles, rank, depth), BF16),
            pltpu.VMEM((na, tiles, part, cols), F32),
            pltpu.VMEM((na, tiles, part, cols), F32),
            dma((nm,)),
            dma((nm,)),
            dma((nm,)),
            dma((na,)),
            dma((na,)),
            dma((na,)),
            dma((na,)),
            dma((nm,)),
            dma((nm,)),
            dma((nm,)),
            dma((nm,)),
            dma((nm,)),
            dma((nm,)),
            dma((nm,)),
            dma((nm,)),
            dma((na,)),
            dma((na,)),
            dma((na,)),
            dma((na,)),
            dma((4,)),
            dma((value_weight.shape[1] // cols,)),
        ],
        compiler_params=pltpu.CompilerParams(
            collective_id=0, has_side_effects=True, vmem_limit_bytes=56 * 1024 * 1024
        ),
    )(tile_adapter, tile_length, adapter_slot, tokens, cotangent, value_weight, down_t, up_store)
    first_t = jnp.swapaxes(down_first[:, 0], 1, 2)
    second_t = jnp.swapaxes(down_second[:, 0], 1, 2)
    outs = pl.pallas_call(
        finish_kernel,
        out_shape=(
            sds((rows, cols), BF16),
            sds((rows, feats), BF16),
            *[sds((slots, rank, depth), F32)] * 3,
            *[sds((slots, part, cols), F32)] * 3,
        ),
        in_specs=[vmem] * 10,
        out_specs=(vmem,) * 8,
        compiler_params=pltpu.CompilerParams(vmem_limit_bytes=60 * 1024 * 1024),
    )(proj, tgrad, gdown, gup, down_t, first_t, second_t, up_store, up_first, up_second)
    back = [jnp.swapaxes(a, 1, 2)[:, None] for a in outs[2:5]]
    return (*outs[:2], *back, *outs[5:])


def by_share(na, nm, *arrays):
    rows, cols = arrays[1].shape
    share = arrays[2].shape[1]
    fits = cols % 128 == 0 and share % cols == 0 and rows % (16 * nm) == 0
    return fused_shards(na, nm, *arrays) if fits else shards(*arrays)


def solution(mesh):
    placed = (
        P("adapter", "mp"),
        P("adapter", "mp"),
        P("mp", "adapter"),
        P(None, "mp", "adapter", None),
        P(None, "mp", "adapter", None),
        P(None, "mp", "adapter", None),
        P(None, "adapter", "mp"),
        P(None, "adapter", "mp"),
        P(None, "adapter", "mp"),
        P(),
        P(),
        P(),
    )
    return jax.shard_map(
        functools.partial(by_share, mesh.shape["adapter"], mesh.shape["mp"]),
        mesh=mesh,
        in_specs=placed,
        out_specs=(
            P("adapter", "mp"),
            P("adapter", "mp"),
            P(None, "mp", "adapter", None),
            P(None, "mp", "adapter", None),
            P(None, "mp", "adapter", None),
            P(None, "adapter", "mp"),
            P(None, "adapter", "mp"),
            P(None, "adapter", "mp"),
        ),
        check_vma=False,
    )
```

```python
import functools

import jax
import jax.numpy as jnp
from jax import lax
from jax.experimental import pallas as pl
from jax.experimental.pallas import tpu as pltpu
from jax.sharding import PartitionSpec as P

TILE = 128
STEP = 100


adapter_scale = 2.0
learn_rate = 0.001
beta_one = 0.9
beta_two = 0.999
adam_eps = 1e-08


def adam_step(store, first, second, gradient):
    new_first = beta_one * first + (1.0 - beta_one) * gradient
    new_second = beta_two * second + (1.0 - beta_two) * gradient * gradient
    corr_one = 1.0 - beta_one**STEP
    corr_two = 1.0 - beta_two**STEP
    moved = store.astype(jnp.float32) - learn_rate * (new_first / corr_one) / (
        jnp.sqrt(new_second / corr_two) + adam_eps
    )
    return (moved, new_first, new_second)


def shards(
    tokens,
    cotangent,
    value_weight,
    down_store,
    down_first,
    down_second,
    up_store,
    up_first,
    up_second,
    tile_adapter,
    tile_length,
    adapter_slot,
):
    tile_total = tile_adapter.shape[0]
    tok_count, feat_part = tokens.shape
    head_cols = cotangent.shape[1]
    tiles_here = tok_count // TILE
    adapter_count = adapter_slot.shape[0]
    my_index = lax.axis_index("adapter")
    adapter_ids = jnp.arange(adapter_count, dtype=jnp.int32)
    tile_adapter_slot = jnp.sum(
        jnp.where(tile_adapter[:, None] == adapter_ids[None, :], adapter_slot[None, :], 0), axis=1
    )
    my_lengths = lax.dynamic_slice_in_dim(tile_length, my_index * tiles_here, tiles_here)
    active_rows = (jnp.arange(TILE)[None, :] < my_lengths[:, None]).reshape(tok_count, 1)
    masked_own = cotangent * active_rows.astype(jnp.bfloat16)
    masked_full = lax.all_gather(masked_own, "mp", axis=1, tiled=True)
    sent_down = down_store[:, 0][tile_adapter_slot]
    sent_up = up_store[tile_adapter_slot]
    down_panel, up_panel = (
        lax.all_to_all(sent_down, "adapter", split_axis=0, concat_axis=1, tiled=True),
        lax.all_to_all(sent_up, "adapter", split_axis=0, concat_axis=1, tiled=True),
    )
    token_tiles = tokens.reshape(tiles_here, TILE, feat_part)
    frozen_part = jnp.dot(
        tokens,
        lax.all_gather(value_weight, "adapter", axis=1, tiled=True),
        preferred_element_type=jnp.float32,
    )
    frozen_local = lax.psum_scatter(frozen_part, "mp", scatter_dimension=1, tiled=True)
    down_part = jnp.einsum(
        "ntd,ndr->ntr", token_tiles, down_panel, preferred_element_type=jnp.float32
    )
    down_sum = lax.psum(down_part, "mp")
    down_portion = down_sum.astype(jnp.bfloat16)
    adapter_term = jnp.einsum(
        "ntr,nrv->ntv", down_portion, up_panel, preferred_element_type=jnp.float32
    ).reshape(tok_count, head_cols)
    projected = (
        (frozen_local + adapter_scale * adapter_term) * active_rows.astype(jnp.float32)
    ).astype(jnp.bfloat16)
    tile_mask = masked_own.reshape(tiles_here, TILE, head_cols)
    backward_piece = adapter_scale * jnp.einsum(
        "ntv,nrv->ntr", tile_mask, up_panel, preferred_element_type=jnp.float32
    )
    backward_portion = lax.psum(backward_piece, "mp").astype(jnp.bfloat16)
    frozen_backward = lax.dot_general(
        masked_full,
        lax.all_gather(value_weight, "adapter", axis=1, tiled=True),
        (((1,), (1,)), ((), ())),
        preferred_element_type=jnp.float32,
    )
    adapter_backward = jnp.einsum(
        "ntr,ndr->ntd", backward_portion, down_panel, preferred_element_type=jnp.float32
    ).reshape(tok_count, feat_part)
    token_gradient = (frozen_backward + adapter_backward).astype(jnp.bfloat16)
    home_down = jnp.einsum(
        "ntd,ntr->ndr", token_tiles, backward_portion, preferred_element_type=jnp.float32
    )
    local_up_weight = adapter_scale * jnp.einsum(
        "ntr,ntv->nrv", down_portion, tile_mask, preferred_element_type=jnp.float32
    )
    arrived_down, arrived_up = (
        lax.all_to_all(home_down, "adapter", split_axis=1, concat_axis=0, tiled=True),
        lax.all_to_all(local_up_weight, "adapter", split_axis=1, concat_axis=0, tiled=True),
    )
    selector = (adapter_ids[:, None] == tile_adapter_slot[None, :]).astype(jnp.float32)
    down_gradient = jnp.dot(
        selector, arrived_down.reshape(tile_total, -1), precision=lax.Precision.HIGHEST
    ).reshape(down_store.shape)
    up_gradient = jnp.dot(
        selector, arrived_up.reshape(tile_total, -1), precision=lax.Precision.HIGHEST
    ).reshape(up_store.shape)
    new_down, new_down_first, new_down_second = adam_step(
        down_store, down_first, down_second, down_gradient
    )
    new_up, new_up_first, new_up_second = adam_step(up_store, up_first, up_second, up_gradient)
    return (
        projected,
        token_gradient,
        new_down,
        new_down_first,
        new_down_second,
        new_up,
        new_up_first,
        new_up_second,
    )


F32 = jnp.float32
BF16 = jnp.bfloat16
NT = (((1,), (1,)), ((), ()))
TN = (((0,), (0,)), ((), ()))


def dot(a, b, dims=(((1,), (0,)), ((), ()))):
    return lax.dot_general(a, b, dims, preferred_element_type=F32)


def fused_kernel(
    na,
    nm,
    tad,
    tlen,
    aslot,
    tok_hbm,
    cot_hbm,
    w,
    down_hbm,
    up_hbm,
    proj,
    tgrad,
    gdown,
    gup,
    tok,
    cot,
    down,
    up,
    wbuf,
    masked,
    sel_d,
    sel_u,
    pan_d,
    pan_u,
    part,
    rs_in,
    db,
    term,
    fro_send,
    fro_recv,
    fro_own,
    acc,
    g_send,
    g_recv,
    gu_send,
    gu_recv,
    wr_s,
    wl_s,
    w_r,
    pd_s,
    pd_r,
    pu_s,
    pu_r,
    ms_s,
    ms_r,
    rs_s,
    rs_r,
    ag_s,
    ag_r,
    fs_s,
    fs_r,
    gd_s,
    gd_r,
    gu_s,
    gu_r,
    load,
    w_load,
):
    z = lax.axis_index("adapter")
    m = lax.axis_index("mp")
    cols = cot.shape[1]
    heads = w.shape[1] // cols
    tiles = tok.shape[0] // TILE
    rank = down.shape[1]
    depth = down.shape[2]
    rank_part = up.shape[1]
    slots = down.shape[0]
    block = tok.shape[0] // nm

    def other_z(d):
        return lax.rem(z + d, na)

    def other_m(d):
        return lax.rem(m + d, nm)

    def remote(src, dst, send, recv, device):
        return pltpu.make_async_remote_copy(
            src_ref=src,
            dst_ref=dst,
            send_sem=send,
            recv_sem=recv,
            device_id=device,
            device_id_type=pl.DeviceIdType.MESH,
        )

    def to_right(g):
        return remote(
            wbuf.at[g], wbuf.at[g], wr_s.at[g], w_r.at[g], {"adapter": lax.rem(z + 1, na)}
        )

    def to_left(g):
        return remote(
            wbuf.at[g], wbuf.at[g], wl_s.at[g], w_r.at[g], {"adapter": lax.rem(z + na - 1, na)}
        )

    def panel_down(src, dst, to):
        return remote(sel_d.at[to], pan_d.at[dst], pd_s.at[to], pd_r.at[src], {"adapter": to})

    def panel_up(src, dst, to):
        return remote(sel_u.at[to], pan_u.at[dst], pu_s.at[to], pu_r.at[src], {"adapter": to})

    def mask_copy(src, to):
        return remote(masked.at[src], masked.at[src], ms_s.at[to], ms_r.at[src], {"mp": to})

    def sum_copy(src, to):
        at = pl.ds(pl.multiple_of(to * block, block), block)
        return remote(part.at[at], rs_in.at[src], rs_s.at[to], rs_r.at[src], {"mp": to})

    def rows_copy(src, to):
        at = pl.ds(pl.multiple_of(src * block, block), block)
        return remote(db.at[at], db.at[at], ag_s.at[to], ag_r.at[src], {"mp": to})

    def frozen_copy(src, to):
        return remote(
            fro_send.at[to], fro_recv.at[src], fs_s.at[to], fs_r.at[src], {"mp": to}
        )

    def grad_down_copy(src, to):
        return remote(g_send.at[to], g_recv.at[src], gd_s.at[to], gd_r.at[src], {"adapter": to})

    def grad_up_copy(src, to):
        return remote(gu_send.at[to], gu_recv.at[src], gu_s.at[to], gu_r.at[src], {"adapter": to})

    loads = [
        pltpu.make_async_copy(src, dst, load.at[i])
        for i, (src, dst) in enumerate(
            ((down_hbm, down), (up_hbm, up), (cot_hbm, cot), (tok_hbm, tok))
        )
    ]
    w_loads = [
        pltpu.make_async_copy(
            w.at[:, pl.ds(h * cols, cols)], wbuf.at[z * heads + h], w_load.at[h]
        )
        for h in range(heads)
    ]
    barrier = pltpu.get_barrier_semaphore()
    for d in range(1, na):
        pl.semaphore_signal(
            barrier, inc=1, device_id={"adapter": other_z(d)}, device_id_type=pl.DeviceIdType.MESH
        )
    for d in range(1, nm):
        pl.semaphore_signal(
            barrier, inc=1, device_id={"mp": other_m(d)}, device_id_type=pl.DeviceIdType.MESH
        )
    for copy in w_loads + loads:
        copy.start()

    slot_of = [aslot[tad[i]] for i in range(na * tiles)]

    def live(n):
        row = lax.broadcasted_iota(jnp.int32, (TILE, cols), 0)
        return jnp.where(row < tlen[z * tiles + n], 1.0, 0.0)

    def send_own(h):
        @pl.when(z < na - 1)
        def _():
            to_right(z * heads + h).start()

        @pl.when(z > 0)
        def _():
            to_left(z * heads + h).start()

    for copy in w_loads:
        copy.wait()
    pl.semaphore_wait(barrier, na + nm - 2)
    send_own(0)

    loads[0].wait()
    loads[1].wait()
    for i in range(na * tiles):
        sel_d[i // tiles, i % tiles] = down[slot_of[i]]
        sel_u[i // tiles, i % tiles] = up[slot_of[i]]
    for d in range(1, na):
        panel_up(z, z, other_z(d)).start()
    for d in range(1, na):
        panel_down(z, z, other_z(d)).start()
    for h in range(1, heads):
        send_own(h)
    loads[2].wait()
    for n in range(tiles):
        at = slice(n * TILE, (n + 1) * TILE)
        masked[m, at] = (cot[at].astype(F32) * live(n)).astype(BF16)
    for d in range(1, nm):
        mask_copy(m, other_m(d)).start()
    pan_d[z] = sel_d[z]
    pan_u[z] = sel_u[z]
    loads[3].wait()

    def forward(g):
        value = dot(tok[...], wbuf[g])

        @pl.when(g == m)
        def _():
            fro_own[...] = value

        @pl.when(g != m)
        def _():
            fro_send[g] = value.astype(BF16)
            frozen_copy(m, g).start()

    def backward(g):
        acc[...] += dot(masked[g], wbuf[g], NT)

    def own_forward(h, carry):
        forward(z * heads + h)
        return carry

    def own_backward(h, carry):
        backward(z * heads + h)
        return carry

    def pass_on(t):
        step = t // heads + 1
        h = lax.rem(t, heads)
        lower = (z - step) * heads + h
        upper = (z + step) * heads + h

        @pl.when(z >= step)
        def _():
            to_right(lower).wait_recv()

            @pl.when(z < na - 1)
            def _():
                to_right(lower).start()

        @pl.when(z + step < na)
        def _():
            to_left(upper).wait_recv()

            @pl.when(z > 0)
            def _():
                to_left(upper).start()

    def multiply(t):
        step = t // heads + 1
        h = lax.rem(t, heads)

        def one(side, inner):
            head = (z + (2 * lax.rem(side, 2) - 1) * step) * heads + h
            valid = jnp.logical_and(head >= 0, head < na * heads)

            @pl.when(jnp.logical_and(valid, side < 2))
            def _():
                forward(head)

            @pl.when(jnp.logical_and(valid, side >= 2))
            def _():
                backward(head)

            return inner

        lax.fori_loop(0, 4, one, 0)

    lax.fori_loop(0, heads, own_forward, 0)
    pass_on(0)

    for d in range(1, na):
        panel_up(other_z(d), z, other_z(d)).wait_recv()
    for d in range(1, na):
        panel_down(other_z(d), other_z(d), other_z(d)).wait_recv()

    def up_panel(n):
        return jnp.concatenate([pan_u[j, n] for j in range(na)], axis=0)

    for n in range(tiles):
        at = slice(n * TILE, (n + 1) * TILE)
        down_part = dot(tok[at, 0:depth], pan_d[0, n], NT)
        for j in range(1, na):
            down_part += dot(tok[at, j * depth : (j + 1) * depth], pan_d[j, n], NT)
        back_part = adapter_scale * dot(masked[m, at], up_panel(n), NT)
        part[at] = jnp.concatenate([down_part, back_part], axis=1)
    for d in range(1, nm):
        sum_copy(m, other_m(d)).start()

    total = part[pl.ds(pl.multiple_of(m * block, block), block)]
    for d in range(1, nm):
        sum_copy(other_m(d), other_m(d)).wait_recv()
        total += rs_in[other_m(d)]
    db[pl.ds(pl.multiple_of(m * block, block), block)] = total.astype(BF16)
    for d in range(1, nm):
        rows_copy(m, other_m(d)).start()

    for d in range(1, nm):
        mask_copy(other_m(d), other_m(d)).wait_recv()
    acc[...] = jnp.zeros_like(acc)
    lax.fori_loop(0, heads, own_backward, 0)
    for d in range(1, nm):
        rows_copy(other_m(d), other_m(d)).wait_recv()

    for n in range(tiles):
        at = slice(n * TILE, (n + 1) * TILE)
        both = db[at]
        down_rows, back_rows = both[:, :rank], both[:, rank:]
        g_tile = dot(back_rows, tok[at], TN)
        gu_tile = adapter_scale * dot(down_rows, masked[m, at], TN)
        for j in range(na):
            g_send[j, n] = g_tile[:, j * depth : (j + 1) * depth].astype(BF16)
            gu_send[j, n] = gu_tile[j * rank_part : (j + 1) * rank_part]
    if heads > 1:
        pass_on(1)
    g_recv[z] = g_send[z]
    gu_recv[z] = gu_send[z]
    for n in range(tiles):
        at = slice(n * TILE, (n + 1) * TILE)
        both = db[at]
        down_rows, back_rows = both[:, :rank], both[:, rank:]
        term[at] = adapter_scale * dot(down_rows, up_panel(n))
        for j in range(na):
            acc[at, j * depth : (j + 1) * depth] += dot(back_rows, pan_d[j, n])

    def sum_slots():
        for d in range(1, na):
            grad_down_copy(other_z(d), other_z(d)).wait_recv()
            grad_up_copy(other_z(d), other_z(d)).wait_recv()

        def slot_sum(s, inner):
            total_d = jnp.zeros((rank, depth), F32)
            total_u = jnp.zeros((rank_part, cols), F32)
            for i in range(na * tiles):
                use = jnp.where(slot_of[i] == s, 1.0, 0.0)
                total_d += use * g_recv[i // tiles, i % tiles].astype(F32)
                total_u += use * gu_recv[i // tiles, i % tiles]
            gdown[s] = total_d
            gup[s] = total_u
            return inner

        lax.fori_loop(0, slots, slot_sum, 0)

    early = min(heads, 2)

    def relay(t, carry):
        @pl.when(t >= early)
        def _():
            pass_on(t)

        @pl.when(t == last_forward)
        def _():
            for d in range(1, na):
                grad_down_copy(z, other_z(d)).start()
                grad_up_copy(z, other_z(d)).start()

        multiply(t)
        return carry

    last_forward = max((na - 2) * heads - 1, 0)
    lax.fori_loop(0, (na - 1) * heads, relay, 0)
    sum_slots()

    tgrad[...] = acc[...].astype(BF16)

    for d in range(1, nm):
        frozen_copy(other_m(d), other_m(d)).wait_recv()
    for n in range(tiles):
        at = slice(n * TILE, (n + 1) * TILE)
        value = fro_own[at] + term[at]
        for d in range(1, nm):
            value += fro_recv[other_m(d), at].astype(F32)
        proj[at] = (value * live(n)).astype(BF16)

    for d in range(1, na):
        panel_up(z, z, other_z(d)).wait_send()
        panel_down(z, z, other_z(d)).wait_send()
        grad_down_copy(z, other_z(d)).wait_send()
        grad_up_copy(z, other_z(d)).wait_send()
    for d in range(1, nm):
        mask_copy(m, other_m(d)).wait_send()
        sum_copy(m, other_m(d)).wait_send()
        rows_copy(m, other_m(d)).wait_send()
        frozen_copy(m, other_m(d)).wait_send()

    def drain(g, carry):
        owner = g // heads

        @pl.when(jnp.logical_and(owner <= z, z < na - 1))
        def _():
            to_right(g).wait_send()

        @pl.when(jnp.logical_and(owner >= z, z > 0))
        def _():
            to_left(g).wait_send()

        return carry

    lax.fori_loop(0, na * heads, drain, 0)


def finish_kernel(proj, tgrad, gdown, gup, down, df, dsec, up, uf, us, *outs):
    outs[0][...] = proj[...]
    outs[1][...] = tgrad[...]
    for i, (store, first, second, grad) in enumerate(
        ((down, df, dsec, gdown), (up, uf, us, gup))
    ):
        for s in range(store.shape[0]):
            values = adam_step(store[s], first[s], second[s], grad[s])
            for k, value in enumerate(values):
                outs[2 + 3 * i + k][s] = value


def fused_shards(
    na,
    nm,
    tokens,
    cotangent,
    value_weight,
    down_store,
    down_first,
    down_second,
    up_store,
    up_first,
    up_second,
    tile_adapter,
    tile_length,
    adapter_slot,
):
    rows, feats = tokens.shape
    cols = cotangent.shape[1]
    tiles = rows // TILE
    slots, _, depth, rank = down_store.shape
    part = up_store.shape[1]
    down_t = jnp.swapaxes(down_store[:, 0], 1, 2)
    vmem = pl.BlockSpec(memory_space=pltpu.VMEM)
    hbm = pl.BlockSpec(memory_space=pltpu.HBM)
    smem = pl.BlockSpec(memory_space=pltpu.SMEM)
    dma = pltpu.SemaphoreType.DMA
    sds = jax.ShapeDtypeStruct
    proj, tgrad, gdown, gup = pl.pallas_call(
        functools.partial(fused_kernel, na, nm),
        out_shape=(
            sds((rows, cols), BF16),
            sds((rows, feats), BF16),
            sds((slots, rank, depth), F32),
            sds((slots, part, cols), F32),
        ),
        in_specs=[smem] * 3 + [hbm] * 5,
        out_specs=(vmem,) * 4,
        scratch_shapes=[
            pltpu.VMEM((rows, feats), BF16),
            pltpu.VMEM((rows, cols), BF16),
            pltpu.VMEM((slots, rank, depth), BF16),
            pltpu.VMEM((slots, part, cols), BF16),
            pltpu.VMEM((nm, feats, cols), BF16),
            pltpu.VMEM((nm, rows, cols), BF16),
            pltpu.VMEM((na, tiles, rank, depth), BF16),
            pltpu.VMEM((na, tiles, part, cols), BF16),
            pltpu.VMEM((na, tiles, rank, depth), BF16),
            pltpu.VMEM((na, tiles, part, cols), BF16),
            pltpu.VMEM((rows, 2 * rank), F32),
            pltpu.VMEM((nm, rows // nm, 2 * rank), F32),
            pltpu.VMEM((rows, 2 * rank), BF16),
            pltpu.VMEM((rows, cols), F32),
            pltpu.VMEM((nm, rows, cols), BF16),
            pltpu.VMEM((nm, rows, cols), BF16),
            pltpu.VMEM((rows, cols), F32),
            pltpu.VMEM((rows, feats), F32),
            pltpu.VMEM((na, tiles, rank, depth), BF16),
            pltpu.VMEM((na, tiles, rank, depth), BF16),
            pltpu.VMEM((na, tiles, part, cols), F32),
            pltpu.VMEM((na, tiles, part, cols), F32),
            dma((nm,)),
            dma((nm,)),
            dma((nm,)),
            dma((na,)),
            dma((na,)),
            dma((na,)),
            dma((na,)),
            dma((nm,)),
            dma((nm,)),
            dma((nm,)),
            dma((nm,)),
            dma((nm,)),
            dma((nm,)),
            dma((nm,)),
            dma((nm,)),
            dma((na,)),
            dma((na,)),
            dma((na,)),
            dma((na,)),
            dma((4,)),
            dma((value_weight.shape[1] // cols,)),
        ],
        compiler_params=pltpu.CompilerParams(
            collective_id=0, has_side_effects=True, vmem_limit_bytes=56 * 1024 * 1024
        ),
    )(tile_adapter, tile_length, adapter_slot, tokens, cotangent, value_weight, down_t, up_store)
    first_t = jnp.swapaxes(down_first[:, 0], 1, 2)
    second_t = jnp.swapaxes(down_second[:, 0], 1, 2)
    outs = pl.pallas_call(
        finish_kernel,
        out_shape=(
            sds((rows, cols), BF16),
            sds((rows, feats), BF16),
            *[sds((slots, rank, depth), F32)] * 3,
            *[sds((slots, part, cols), F32)] * 3,
        ),
        in_specs=[vmem] * 10,
        out_specs=(vmem,) * 8,
        compiler_params=pltpu.CompilerParams(vmem_limit_bytes=60 * 1024 * 1024),
    )(proj, tgrad, gdown, gup, down_t, first_t, second_t, up_store, up_first, up_second)
    back = [jnp.swapaxes(a, 1, 2)[:, None] for a in outs[2:5]]
    return (*outs[:2], *back, *outs[5:])


def by_share(na, nm, *arrays):
    rows, cols = arrays[1].shape
    share = arrays[2].shape[1]
    fits = cols % 128 == 0 and share % cols == 0 and rows % (16 * nm) == 0
    return fused_shards(na, nm, *arrays) if fits else shards(*arrays)


def solution(mesh):
    placed = (
        P("adapter", "mp"),
        P("adapter", "mp"),
        P("mp", "adapter"),
        P(None, "mp", "adapter", None),
        P(None, "mp", "adapter", None),
        P(None, "mp", "adapter", None),
        P(None, "adapter", "mp"),
        P(None, "adapter", "mp"),
        P(None, "adapter", "mp"),
        P(),
        P(),
        P(),
    )
    return jax.shard_map(
        functools.partial(by_share, mesh.shape["adapter"], mesh.shape["mp"]),
        mesh=mesh,
        in_specs=placed,
        out_specs=(
            P("adapter", "mp"),
            P("adapter", "mp"),
            P(None, "mp", "adapter", None),
            P(None, "mp", "adapter", None),
            P(None, "mp", "adapter", None),
            P(None, "adapter", "mp"),
            P(None, "adapter", "mp"),
            P(None, "adapter", "mp"),
        ),
        check_vma=False,
    )
```
